32 devices in a mesh: seq: 8 (over z, y), head: 4 (over x, core).
Axes of the slice: x: 2, y: 2, z: 4, core: 2. Of those that a mesh axis runs over, the one named last changes fastest.
Arguments:
- queries: bfloat16 [1024, 3072], P('seq', 'head'), may hold values from -2 to 2
- key_rows: bfloat16 [1024, 3072], P('seq', 'head'), may hold values from -2 to 2
- values: bfloat16 [1024, 3072], P('seq', 'head'), may hold values from -6 to 6
- conv_input: bfloat16 [1024, 3072], P('seq', 'head'), may hold values from -0.14941406 to 0.14941406
- log_gates: bfloat16 [1024, 3072], P('seq', 'head'), may hold values from -1 to 0
- grad_output: bfloat16 [1024, 3072], P('seq', 'head'), may hold values from -0.8984375 to 0.8984375
- saved_state: float32 [8, 24, 128, 128], P('seq', 'head'), may hold values from -6 to 6
- conv_kernel: float32 [4, 3072], replicated, may hold values from -3 to 3
Outputs:
- grad_queries: bfloat16 [1024, 3072], P('seq', 'head')
- grad_keys: bfloat16 [1024, 3072], P('seq', 'head')
- grad_gates: bfloat16 [1024, 3072], P('seq', 'head')
- grad_input: bfloat16 [1024, 3072], P(('seq', 'head'))
- grad_kernel: float32 [4, 3072], P(None, 'head')
The draws below stay inside these ranges and needn't reach their ends.
All inputs are finite; a program needn't handle non-finite values.
Results may differ from the reference program's by a relative error of at most 0.0049.
Values may be sent and summed in bfloat16 or wider, within the bound.
A program may use at most 64 MiB of HBM per device.

```python
import math
import jax
import jax.numpy as jnp
from jax import lax

HEADS = 24
DK = 128
DV = 128
STRETCH = 64
KW = 4
TOK_DEV = 128
SPAN_POSITIONS = 1024
BLOCKS = 8


def channel_rates(key):
    pick_key, slow_key, fast_key = jax.random.split(jax.random.fold_in(key, 7), 3)
    width = HEADS * DK
    share = 0.5
    fast = jax.random.uniform(pick_key, (width,)) < share
    slow_rate = jnp.exp(jax.random.uniform(slow_key, (width,), minval=math.log(0.05), maxval=math.log(0.5))) / SPAN_POSITIONS
    quick_decay_rate = jnp.exp(jax.random.uniform(fast_key, (width,), minval=math.log(1.0 / 50.0), maxval=math.log(1.0 / 30.0)))
    return jnp.where(fast, quick_decay_rate, slow_rate)


def scaled_rows(key, salt):
    fading_speeds = channel_rates(key)
    noise_key = jax.random.fold_in(jax.random.fold_in(key, salt), 0)
    shape = (SPAN_POSITIONS, HEADS * DK)
    noise = jnp.clip(jax.random.normal(noise_key, shape), -6.0, 6.0)
    return (noise * jnp.sqrt(2.0 * fading_speeds)[None, :]).astype(jnp.bfloat16)


def draw_queries(key, part):
    return scaled_rows(key, 21)


def draw_key_rows(key, part):
    return scaled_rows(key, 22)


def draw_log_gates(key, part):
    fading_speeds = channel_rates(key)
    width = HEADS * DK
    blocks = SPAN_POSITIONS // TOK_DEV
    mod_key, rough_key, place_key, loss_key = jax.random.split(jax.random.fold_in(key, 11), 4)
    scaling_multiplier = jnp.repeat(jnp.exp(jax.random.uniform(mod_key, (blocks, width), minval=-0.7, maxval=0.7)), TOK_DEV, axis=0)
    coarse_perturbation = jnp.exp(jax.random.uniform(rough_key, (SPAN_POSITIONS, width), minval=math.log(0.5), maxval=math.log(1.5)))
    position_offsets = jax.random.randint(place_key, (3,), 0, SPAN_POSITIONS)
    spike_amplitudes = jnp.any(jnp.arange(SPAN_POSITIONS)[:, None] == position_offsets[None, :], axis=1)
    objective_scores = jnp.log(jax.random.uniform(loss_key, (SPAN_POSITIONS, width), minval=0.6, maxval=0.8))
    forgetting_levels = -fading_speeds[None, :] * coarse_perturbation * scaling_multiplier + jnp.where(spike_amplitudes[:, None], objective_scores, 0.0)
    return forgetting_levels.astype(jnp.bfloat16)


def level_of(key, shape, pieces, smallest, top_value):
    loudness, own = 1.0, jax.random.fold_in(key, 6)
    for axis_at, parts in pieces:
        heights = jnp.exp(jax.random.uniform(jax.random.fold_in(own, axis_at), (parts,), jnp.float32, smallest / len(pieces), top_value / len(pieces)))
        loudness = loudness * jnp.repeat(heights, shape[axis_at] // parts).reshape([-1 if axis == axis_at else 1 for axis in range(len(shape))])
    return loudness


def bell_draw(rng, extent, scale, limit, pieces=(), dtype=jnp.bfloat16):
    entries = scale * jax.random.normal(rng, extent, jnp.float32)
    if pieces:
        entries = entries * level_of(rng, extent, pieces, -0.22, 0.18)
    return jnp.clip(entries, -limit, limit).astype(dtype)


def setup_inputs(seed: int = 0) -> dict:
    key_list = jax.random.split(jax.random.key(seed), 9)
    return {
        "queries": draw_queries(jax.random.fold_in(key_list[8], 71), 0),
        "key_rows": draw_key_rows(jax.random.fold_in(key_list[8], 71), 0),
        "values": bell_draw(key_list[2], (SPAN_POSITIONS, HEADS * DV), 1.0, 6.0, ((0, 8), (1, 4))),
        "conv_input": bell_draw(key_list[3], (SPAN_POSITIONS, HEADS * DV), 0.025, 0.14941406, ((0, 8), (1, 4))),
        "log_gates": draw_log_gates(jax.random.fold_in(key_list[8], 71), 0),
        "grad_output": bell_draw(key_list[5], (SPAN_POSITIONS, HEADS * DV), 0.15, 0.8984375, ((0, 8), (1, 4))),
        "saved_state": bell_draw(key_list[6], (BLOCKS, HEADS, DK, DV), 1.0, 6.0, ((0, 8), (1, 4)), jnp.float32),
        "conv_kernel": bell_draw(key_list[7], (KW, HEADS * DV), 0.5, 3.0, (), jnp.float32),
    }


PRECISE = lax.Precision.HIGHEST

def shard_pass(queries, key_rows, values, log_gates, grad_out, start_state, incoming):
    length = queries.shape[0]
    stretches = length // STRETCH
    query_c = queries.reshape((stretches, STRETCH) + queries.shape[1:])
    key_c = key_rows.reshape((stretches, STRETCH) + key_rows.shape[1:])
    value_c = values.reshape((stretches, STRETCH) + values.shape[1:])
    grad_c = grad_out.reshape((stretches, STRETCH) + grad_out.shape[1:])
    within = jnp.cumsum(log_gates.reshape((stretches, STRETCH) + log_gates.shape[1:]), axis=1)
    running_totals = within[:, -1]
    query_up = query_c * jnp.exp(within)
    key_down = key_c * jnp.exp(-within)
    key_tail = key_c * jnp.exp(running_totals[:, None] - within)
    growth = jnp.einsum('ntha,nthe->nhae', key_tail, value_c, precision=PRECISE)

    def step_forward(current, inputs):
        decays, addend = inputs
        return (jnp.exp(decays)[..., None] * current + addend, current)
    last_state, starts = lax.scan(step_forward, start_state, (running_totals, growth))
    pushes = jnp.einsum('ntha,nthe->nhae', query_up, grad_c, precision=PRECISE)
    leaving, stretch_ends = lax.scan(step_forward, incoming, (running_totals, pushes), reverse=True)
    steps_idx = jnp.arange(STRETCH)
    lower_mask = (steps_idx[:, None] >= steps_idx[None, :]).astype(jnp.float32)
    scores = jnp.einsum('nthe,nshe->nhts', grad_c, value_c, precision=PRECISE) * lower_mask
    grad_query = jnp.exp(within) * (jnp.einsum('nthe,nhae->ntha', grad_c, starts, precision=PRECISE) + jnp.einsum('nhts,nsha->ntha', scores, key_down, precision=PRECISE))
    grad_key = jnp.exp(-within) * jnp.einsum('nhts,ntha->nsha', scores, query_up, precision=PRECISE) + jnp.exp(running_totals[:, None] - within) * jnp.einsum('nshe,nhae->nsha', value_c, stretch_ends, precision=PRECISE)
    weights = jnp.einsum('nsha,ntha->nhst', key_down, query_up, precision=PRECISE) * lower_mask.T
    grad_value = jnp.einsum('nhst,nthe->nshe', weights, grad_c, precision=PRECISE) + jnp.einsum('nsha,nhae->nshe', key_tail, stretch_ends, precision=PRECISE)
    return (grad_query.reshape(queries.shape), grad_key.reshape(key_rows.shape), grad_value.reshape(values.shape), last_state, leaving)

def gate_grad(queries, grad_query, key_rows, grad_key, incoming, last_state):
    terms = queries * grad_query - key_rows * grad_key
    backward_sum = jnp.cumsum(terms[::-1], axis=0)[::-1]
    return backward_sum + lax.optimization_barrier(jnp.sum(incoming * last_state, axis=-1))[None]

def reference(queries, key_rows, values, conv_input, log_gates, grad_output, saved_state, conv_kernel):
    columns = HEADS * DV

    def blocked(array, width):
        return array.reshape(BLOCKS, TOK_DEV, HEADS, width)

    def step(running, inputs):
        incoming, next_rows, kernel_accumulated_sum = running
        query_b, key_b, value_b, input_b, gate_b, grad_b, start_b = inputs
        query_f = query_b.astype(jnp.float32)
        key_f = key_b.astype(jnp.float32)
        grad_query, grad_key, grad_value, last_state, leaving = shard_pass(query_f, key_f, value_b.astype(jnp.float32), gate_b.astype(jnp.float32), grad_b.astype(jnp.float32), start_b, incoming)
        grad_gate = gate_grad(query_f, grad_query, key_f, grad_key, incoming, last_state)
        rounded = lax.optimization_barrier(grad_value.reshape(TOK_DEV, columns).astype(jnp.bfloat16)).astype(jnp.float32)
        padded = jnp.concatenate([rounded, next_rows], axis=0)
        input_f = input_b.astype(jnp.float32)
        conv_grad = jnp.zeros((TOK_DEV, columns), jnp.float32)
        tap_terms = []
        for tap_index in range(KW):
            window = padded[tap_index:tap_index + TOK_DEV]
            conv_grad = conv_grad + conv_kernel[tap_index] * window
            tap_terms.append(lax.optimization_barrier(jnp.sum(input_f * window, axis=0)))
        outputs = (grad_query.reshape(TOK_DEV, HEADS * DK).astype(jnp.bfloat16), grad_key.reshape(TOK_DEV, HEADS * DK).astype(jnp.bfloat16), grad_gate.reshape(TOK_DEV, HEADS * DK).astype(jnp.bfloat16), conv_grad.astype(jnp.bfloat16))
        return ((leaving, rounded[:KW - 1], kernel_accumulated_sum + jnp.stack(tap_terms)), outputs)
    initial = (jnp.zeros((HEADS, DK, DV), jnp.float32), jnp.zeros((KW - 1, columns), jnp.float32), jnp.zeros((KW, columns), jnp.float32))
    inputs = (blocked(queries, DK), blocked(key_rows, DK), blocked(values, DV), conv_input.reshape(BLOCKS, TOK_DEV, columns), blocked(log_gates, DK), blocked(grad_output, DV), saved_state)
    final, stacked = lax.scan(step, initial, inputs, reverse=True)
    grad_queries = stacked[0].reshape(SPAN_POSITIONS, HEADS * DK)
    grad_keys = stacked[1].reshape(SPAN_POSITIONS, HEADS * DK)
    grad_gates = stacked[2].reshape(SPAN_POSITIONS, HEADS * DK)
    grad_input = stacked[3].reshape(SPAN_POSITIONS, columns)
    return (grad_queries, grad_keys, grad_gates, grad_input, final[2])
```

```python
import functools

import jax
import jax.numpy as jnp
from jax import lax
from jax.experimental import pallas as pl
from jax.experimental.pallas import tpu as pltpu
from jax.sharding import PartitionSpec as P

MESH = pl.DeviceIdType.MESH
F32 = jnp.float32
BF16 = jnp.bfloat16
LANES = 128
EDGE = 16


def product(a, b, dim_a, dim_b):
    return lax.dot_general(
        a, b, (((dim_a,), (dim_b,)), ((), ())), preferred_element_type=F32
    )


def halves(x):
    high = x.astype(BF16)
    return high, (x - high.astype(F32)).astype(BF16)


def both(x, axis):
    return jnp.concatenate(halves(x), axis=axis)


def twice(x, axis):
    return jnp.concatenate([x, x], axis=axis)


def body(
    seqs, groups, inner, heads, tokens, taps,
    q_in, k_in, v_in, x_in, l_in, g_in, s_in, w_in,
    gq_out, gk_out, gg_out, gi_out, gw_out,
    q, k, v, x, l, g, s, w,
    c, qup, kdn, scale, ktail, terms, gk_part, gv_part, gg_part,
    push, dec, gath, dgath, alone, decays, carry, leave, ends, incoming,
    gq_b, gk_b, gg_b, gv, gi, sums, all_sums,
    in_sem, out_sem, push_s, push_r, dec_s, dec_r, hop_s, hop_r, end_s, end_r,
    edge_s, edge_r, row_s, row_r, sum_s, sum_r,
):
    p = lax.axis_index("seq")
    hd = lax.axis_index("head")
    o, i = p // inner, p % inner
    outer = seqs // inner
    part = LANES // inner
    columns = heads * LANES
    own_rows = tokens // groups
    cols = [slice(h * LANES, (h + 1) * LANES) for h in range(heads)]

    mine = pl.ds(pl.multiple_of(hd * columns, LANES), columns)
    loads = [
        pltpu.make_async_copy(src, dst, in_sem.at[n])
        for n, (src, dst) in enumerate(
            [(l_in, l), (q_in, q), (g_in, g), (k_in, k), (v_in, v), (s_in.at[0], s), (x_in, x), (w_in.at[:, mine], w)]
        )
    ]
    for load in loads:
        load.start()

    def greet(n, carried):
        pl.semaphore_signal(
            barrier, inc=1, device_id=(lax.rem(p + n, seqs), hd), device_id_type=MESH
        )
        return carried

    barrier = pltpu.get_barrier_semaphore()
    lax.fori_loop(1, seqs, greet, 0)
    for n in range(1, groups):
        pl.semaphore_signal(
            barrier, inc=1, device_id=(p, lax.rem(hd + n, groups)), device_id_type=MESH
        )

    row = lax.broadcasted_iota(jnp.int32, (tokens, tokens), 0)
    col = lax.broadcasted_iota(jnp.int32, (tokens, tokens), 1)
    lower = row >= col
    upper = col >= row
    lower_b = jnp.where(lower, 1.0, 0.0).astype(BF16)
    upper_b = jnp.where(upper, 1.0, 0.0).astype(BF16)
    strict_b = jnp.where(row > col, 1.0, 0.0).astype(BF16)

    loads[0].wait()
    total = product(lower_b, l[...], 1, 0)
    c[...] = total
    middle = total[tokens // 2 - 1 : tokens // 2]
    last = total[tokens - 1 : tokens]
    to_middle = jnp.exp(middle)
    grow = jnp.exp(total - middle)
    whole = jnp.exp(last)
    for h in range(heads):
        dec[h] = jnp.broadcast_to(whole[:, cols[h]], (8, LANES))
    loads[1].wait()
    up = q[...].astype(F32) * grow
    qup[...] = up.astype(BF16)
    full = up * to_middle
    loads[2].wait()
    for h in range(heads):
        push[h] = product(twice(g[:, cols[h]], 0), both(full[:, cols[h]], 0), 0, 0).astype(BF16)

    pl.semaphore_wait(barrier, seqs - 1 + groups - 1)

    def push_copy(sender, to):
        return pltpu.make_async_remote_copy(
            src_ref=push.at[:, to * part : (to + 1) * part, :],
            dst_ref=gath.at[sender],
            send_sem=push_s.at[to],
            recv_sem=push_r.at[sender],
            device_id=(o * inner + to, hd),
            device_id_type=MESH,
        )

    def dec_copy(sender, to):
        return pltpu.make_async_remote_copy(
            src_ref=dec,
            dst_ref=dgath.at[sender],
            send_sem=dec_s.at[to],
            recv_sem=dec_r.at[sender],
            device_id=(o * inner + to, hd),
            device_id_type=MESH,
        )

    for j in range(inner):

        @pl.when(j != i)
        def _(j=j):
            push_copy(i, j).start()
            dec_copy(i, j).start()

    gath[i] = push[:, pl.ds(pl.multiple_of(i * part, part), part), :]
    dgath[i] = dec[...]

    loads[3].wait()
    loads[4].wait()
    loads[5].wait()
    total = c[...]
    middle = total[tokens // 2 - 1 : tokens // 2]
    last = total[tokens - 1 : tokens]
    down = k[...].astype(F32) * jnp.exp(middle - total)
    kdn[...] = down.astype(BF16)
    scale[...] = jnp.exp(last - total)
    ktail[...] = down * jnp.exp(last - middle)
    scores = []
    for h in range(heads):
        at = cols[h]
        g_h = g[:, at]
        score = jnp.where(lower, product(g_h, v[:, at], 1, 1), 0.0).astype(BF16)
        scores.append(score)
        total = c[:, at]
        middle = total[tokens // 2 - 1 : tokens // 2]
        from_start = product(twice(g_h, 1), both(s[h], 1), 1, 1) * jnp.exp(total)
        kdn_h = kdn[:, at]
        qup_h = qup[:, at]
        inside = product(score, kdn_h, 1, 0)
        back = product(score, qup_h, 0, 0)
        gq_b[:, at] = (jnp.exp(total - middle) * inside + from_start).astype(BF16)
        gk_part[:, at] = jnp.exp(middle - total) * back
        terms[:, at] = (
            qup_h.astype(F32) * inside - kdn_h.astype(F32) * back + q[:, at].astype(F32) * from_start
        )
    save_q = pltpu.make_async_copy(gq_b, gq_out, out_sem.at[0])
    save_q.start()

    for j in range(inner):

        @pl.when(j != i)
        def _(j=j):
            push_copy(j, j).wait_recv()
            dec_copy(j, j).wait_recv()

    for h in range(heads):
        state = gath[inner - 1, h].astype(F32)
        decay = dgath[inner - 1, h, 0:1]
        for j in range(inner - 2, -1, -1):
            alone[j, h] = state
            decays[j, h] = jnp.broadcast_to(decay, (8, LANES))
            step = dgath[j, h, 0:1]
            state = gath[j, h].astype(F32) + step * state
            decay = decay * step
        alone[inner - 1, h] = state
        decays[inner - 1, h] = jnp.broadcast_to(decay, (8, LANES))

    def hop_copy():
        return pltpu.make_async_remote_copy(
            src_ref=leave,
            dst_ref=carry,
            send_sem=hop_s,
            recv_sem=hop_r,
            device_id=(p - inner, hd),
            device_id_type=MESH,
        )

    @pl.when(o == outer - 1)
    def _():
        carry[...] = jnp.zeros_like(carry)

    if outer > 1:

        @pl.when(o < outer - 1)
        def _():
            hop_copy().wait_recv()

        @pl.when(o > 0)
        def _():
            for h in range(heads):
                leave[h] = (
                    alone[inner - 1, h] + decays[inner - 1, h, 0:1] * carry[h].astype(F32)
                ).astype(BF16)
            hop_copy().start()

    for h in range(heads):
        from_later = carry[h].astype(F32)
        ends[inner - 1, h] = carry[h]
        for j in range(inner - 1):
            ends[j, h] = (alone[j, h] + decays[j, h, 0:1] * from_later).astype(BF16)

    share = pl.ds(pl.multiple_of(i * part, part), part)

    def end_copy(sender, to, where):
        return pltpu.make_async_remote_copy(
            src_ref=ends.at[to],
            dst_ref=incoming.at[:, where, :],
            send_sem=end_s.at[to],
            recv_sem=end_r.at[sender],
            device_id=(o * inner + to, hd),
            device_id_type=MESH,
        )

    for j in range(inner):

        @pl.when(j != i)
        def _(j=j):
            end_copy(i, j, share).start()

    incoming[:, share, :] = ends[i]

    for h in range(heads):
        at = cols[h]
        total = c[:, at]
        middle = total[tokens // 2 - 1 : tokens // 2]
        k_high, k_low = halves(k[:, at].astype(F32) * jnp.exp(middle - total))
        q_high, q_low = halves(q[:, at].astype(F32) * jnp.exp(total - middle))
        weight = product(
            jnp.concatenate([k_high, k_high], axis=1), jnp.concatenate([q_high, q_low], axis=1), 1, 1
        ) + product(k_low, q_high, 1, 1)
        weight = jnp.where(upper, weight, 0.0)
        gv_part[:, at] = product(both(weight, 1), twice(g[:, at], 0), 1, 0)
    gg_part[...] = product(twice(upper_b, 1), both(terms[...], 0), 1, 0)

    for j in range(inner):

        @pl.when(j != i)
        def _(j=j):
            end_copy(j, j, slice(j * part, (j + 1) * part)).wait_recv()

    for h in range(heads):
        at = cols[h]
        gv[0:tokens, at] = (
            gv_part[:, at] + product(both(ktail[:, at], 1), twice(incoming[h], 1), 1, 1)
        ).astype(BF16)

    def edge_copy():
        return pltpu.make_async_remote_copy(
            src_ref=gv.at[0:EDGE],
            dst_ref=gv.at[tokens : tokens + EDGE],
            send_sem=edge_s,
            recv_sem=edge_r,
            device_id=(p - 1, hd),
            device_id_type=MESH,
        )

    @pl.when(p > 0)
    def _():
        edge_copy().start()

    @pl.when(p == seqs - 1)
    def _():
        gv[tokens : tokens + EDGE] = jnp.zeros((EDGE, columns), BF16)

    loads[6].wait()
    loads[7].wait()

    def convolve(first, end):
        rows = gv[first : end + EDGE].astype(F32)
        result = w[0:1] * rows[: end - first]
        for tap in range(1, taps):
            result = result + w[tap : tap + 1] * rows[tap : tap + end - first]
        gi[first:end] = result.astype(BF16)

    def row_copy(sender, to):
        return pltpu.make_async_remote_copy(
            src_ref=gi.at[to * own_rows : (to + 1) * own_rows],
            dst_ref=gi_out.at[:, pl.ds(pl.multiple_of(sender * columns, LANES), columns)],
            send_sem=row_s.at[to],
            recv_sem=row_r.at[sender],
            device_id=(p, to),
            device_id_type=MESH,
        )

    def keep_copy(to):
        return pltpu.make_async_copy(
            gi.at[to * own_rows : (to + 1) * own_rows], gi_out.at[:, mine], row_s.at[to]
        )

    def hand_out(to):
        @pl.when(to != hd)
        def _():
            row_copy(hd, to).start()

        @pl.when(to == hd)
        def _():
            keep_copy(to).start()

    for to in range(groups - 1):
        convolve(to * own_rows, (to + 1) * own_rows)
        hand_out(to)

    @pl.when(p < seqs - 1)
    def _():
        edge_copy().wait_recv()

    convolve((groups - 1) * own_rows, tokens)
    hand_out(groups - 1)

    rows = gv[...].astype(F32)
    x_f = x[...].astype(F32)
    sums[...] = jnp.zeros_like(sums)
    for tap in range(taps):
        sums[tap : tap + 1] = jnp.sum(x_f * rows[tap : tap + tokens], axis=0, keepdims=True)

    def sum_copy(sender, to):
        return pltpu.make_async_remote_copy(
            src_ref=sums,
            dst_ref=all_sums.at[sender],
            send_sem=sum_s.at[to],
            recv_sem=sum_r.at[sender],
            device_id=(to, hd),
            device_id_type=MESH,
        )

    def send_sum(n, carried):
        sum_copy(p, lax.rem(p + n, seqs)).start()
        return carried

    lax.fori_loop(1, seqs, send_sum, 0)
    all_sums[p] = sums[...]

    new_terms = []
    for h in range(heads):
        at = cols[h]
        later = product(v[:, at], incoming[h], 1, 0)
        gk_b[:, at] = (gk_part[:, at] + scale[:, at] * later).astype(BF16)
        own = jnp.sum(incoming[h].astype(F32) * s[h].T, axis=0, keepdims=True)
        gg = (
            gg_part[:, at]
            + product(strict_b, (ktail[:, at] * later).astype(BF16), 1, 0)
            + own * dec[h, 0:1]
        )
        gg_b[:, at] = gg.astype(BF16)
    save_k = pltpu.make_async_copy(gk_b, gk_out, out_sem.at[1])
    save_g = pltpu.make_async_copy(gg_b, gg_out, out_sem.at[2])
    save_k.start()
    save_g.start()

    def take_sum(n, carried):
        other = lax.rem(p + n, seqs)
        sum_copy(other, other).wait_recv()
        return carried

    lax.fori_loop(1, seqs, take_sum, 0)
    added = lax.fori_loop(
        0, seqs, lambda n, value: value + all_sums[n], jnp.zeros((8, columns), F32)
    )
    sums_out = w
    sums_out[...] = added[:taps]
    save_w = pltpu.make_async_copy(sums_out, gw_out, out_sem.at[3])
    save_w.start()

    for sender in range(groups):

        @pl.when(sender != hd)
        def _(sender=sender):
            row_copy(sender, sender).wait_recv()

    for to in range(groups):

        @pl.when(to != hd)
        def _(to=to):
            row_copy(hd, to).wait_send()

        @pl.when(to == hd)
        def _(to=to):
            keep_copy(to).wait()

    def sent_sum(n, carried):
        sum_copy(p, lax.rem(p + n, seqs)).wait_send()
        return carried

    lax.fori_loop(1, seqs, sent_sum, 0)
    for j in range(inner):

        @pl.when(j != i)
        def _(j=j):
            push_copy(i, j).wait_send()
            dec_copy(i, j).wait_send()
            end_copy(i, j, share).wait_send()

    if outer > 1:

        @pl.when(o > 0)
        def _():
            hop_copy().wait_send()

    @pl.when(p > 0)
    def _():
        edge_copy().wait_send()

    for save in (save_q, save_k, save_g, save_w):
        save.wait()


def solution(mesh):
    seqs, groups = mesh.shape["seq"], mesh.shape["head"]
    inner = 4 if seqs % 4 == 0 else 1

    def per_device(queries, key_rows, values, conv_input, log_gates, grad_output, saved_state, conv_kernel):
        tokens, columns = queries.shape
        heads = saved_state.shape[1]
        taps = conv_kernel.shape[0]
        part = LANES // inner
        flat = (tokens, columns)
        dma = pltpu.SemaphoreType.DMA
        vmem = pltpu.VMEM
        return pl.pallas_call(
            functools.partial(body, seqs, groups, inner, heads, tokens, taps),
            out_shape=(
                jax.ShapeDtypeStruct(flat, BF16),
                jax.ShapeDtypeStruct(flat, BF16),
                jax.ShapeDtypeStruct(flat, BF16),
                jax.ShapeDtypeStruct((tokens // groups, columns * groups), BF16),
                jax.ShapeDtypeStruct((taps, columns), F32),
            ),
            in_specs=[pl.BlockSpec(memory_space=pl.ANY)] * 8,
            out_specs=[pl.BlockSpec(memory_space=pl.ANY)] * 5,
            scratch_shapes=[vmem(flat, BF16)] * 6
            + [
                vmem((heads, LANES, LANES), F32),
                vmem((taps, columns), F32),
                vmem(flat, F32),
                vmem(flat, BF16),
                vmem(flat, BF16),
                vmem(flat, F32),
                vmem(flat, F32),
                vmem(flat, F32),
                vmem(flat, F32),
                vmem(flat, F32),
                vmem(flat, F32),
                vmem((heads, LANES, LANES), BF16),
                vmem((heads, 8, LANES), F32),
                vmem((inner, heads, part, LANES), BF16),
                vmem((inner, heads, 8, LANES), F32),
                vmem((inner, heads, part, LANES), F32),
                vmem((inner, heads, 8, LANES), F32),
                vmem((heads, part, LANES), BF16),
                vmem((heads, part, LANES), BF16),
                vmem((inner, heads, part, LANES), BF16),
                vmem((heads, LANES, LANES), BF16),
                vmem(flat, BF16),
                vmem(flat, BF16),
                vmem(flat, BF16),
                vmem((tokens + EDGE, columns), BF16),
                vmem(flat, BF16),
                vmem((8, columns), F32),
                vmem((seqs, 8, columns), F32),
                dma((8,)),
                dma((4,)),
                dma((inner,)),
                dma((inner,)),
                dma((inner,)),
                dma((inner,)),
                dma,
                dma,
                dma((inner,)),
                dma((inner,)),
                dma,
                dma,
                dma((groups,)),
                dma((groups,)),
                dma((seqs,)),
                dma((seqs,)),
            ],
            compiler_params=pltpu.CompilerParams(
                collective_id=0, has_side_effects=True, vmem_limit_bytes=32 * 1024 * 1024
            ),
        )(queries, key_rows, values, conv_input, log_gates, grad_output, saved_state, conv_kernel)

    return jax.shard_map(
        per_device,
        mesh=mesh,
        in_specs=(
            P("seq", "head"),
            P("seq", "head"),
            P("seq", "head"),
            P("seq", "head"),
            P("seq", "head"),
            P("seq", "head"),
            P("seq", "head", None, None),
            P(),
        ),
        out_specs=(
            P("seq", "head"),
            P("seq", "head"),
            P("seq", "head"),
            P(("seq", "head"), None),
            P(None, "head"),
        ),
        check_vma=False,
    )
```

```python
import functools

import jax
import jax.numpy as jnp
from jax import lax
from jax.experimental import pallas as pl
from jax.experimental.pallas import tpu as pltpu
from jax.sharding import PartitionSpec as P

MESH = pl.DeviceIdType.MESH
F32 = jnp.float32
BF16 = jnp.bfloat16
LANES = 128
EDGE = 16


def product(a, b, dim_a, dim_b):
    return lax.dot_general(
        a, b, (((dim_a,), (dim_b,)), ((), ())), preferred_element_type=F32
    )


def halves(x):
    high = x.astype(BF16)
    return high, (x - high.astype(F32)).astype(BF16)


def both(x, axis):
    return jnp.concatenate(halves(x), axis=axis)


def twice(x, axis):
    return jnp.concatenate([x, x], axis=axis)


def body(
    seqs, groups, inner, heads, tokens, taps,
    q_in, k_in, v_in, x_in, l_in, g_in, s_in, w_in,
    gq_out, gk_out, gg_out, gi_out, gw_out,
    q, k, v, x, l, g, s, w,
    turned, tails, c, qup, kdn, scale, ktail, terms, gk_part, gv_part, gg_part,
    push, dec, gath, dgath, alone, decays, carry, leave, ends, incoming,
    gv, gi, sums, all_sums,
    in_sem, push_s, push_r, dec_s, dec_r, hop_s, hop_r, end_s, end_r,
    edge_s, edge_r, row_s, row_r, sum_s, sum_r,
):
    p = lax.axis_index("seq")
    hd = lax.axis_index("head")
    o, i = p // inner, p % inner
    outer = seqs // inner
    part = LANES // inner
    columns = heads * LANES
    own_rows = tokens // groups
    cols = [slice(h * LANES, (h + 1) * LANES) for h in range(heads)]

    mine = pl.ds(pl.multiple_of(hd * columns, LANES), columns)
    loads = [
        pltpu.make_async_copy(src, dst, in_sem.at[n])
        for n, (src, dst) in enumerate(
            [(l_in, l), (q_in, q), (g_in, g), (k_in, k), (v_in, v), (s_in.at[0], s), (x_in, x), (w_in.at[:, mine], w)]
        )
    ]
    for load in loads:
        load.start()

    def greet(n, carried):
        pl.semaphore_signal(
            barrier, inc=1, device_id=(lax.rem(p + n, seqs), hd), device_id_type=MESH
        )
        return carried

    barrier = pltpu.get_barrier_semaphore()
    lax.fori_loop(1, seqs, greet, 0)
    for n in range(1, groups):
        pl.semaphore_signal(
            barrier, inc=1, device_id=(p, lax.rem(hd + n, groups)), device_id_type=MESH
        )

    row = lax.broadcasted_iota(jnp.int32, (tokens, tokens), 0)
    col = lax.broadcasted_iota(jnp.int32, (tokens, tokens), 1)
    lower = row >= col
    upper = col >= row
    lower_b = jnp.where(lower, 1.0, 0.0).astype(BF16)
    upper_b = jnp.where(upper, 1.0, 0.0).astype(BF16)
    strict_b = jnp.where(row > col, 1.0, 0.0).astype(BF16)

    loads[0].wait()
    total = product(lower_b, l[...], 1, 0)
    c[...] = total
    middle = total[tokens // 2 - 1 : tokens // 2]
    last = total[tokens - 1 : tokens]
    to_middle = jnp.exp(middle)
    grow = jnp.exp(total - middle)
    whole = jnp.exp(last)
    for h in range(heads):
        dec[h : h + 1] = whole[:, cols[h]]
    loads[1].wait()
    up = q[...].astype(F32) * grow
    qup[...] = up.astype(BF16)
    full = up * to_middle
    loads[2].wait()
    for h in range(heads):
        push[h] = product(twice(g[:, cols[h]], 0), both(full[:, cols[h]], 0), 0, 0).astype(BF16)

    pl.semaphore_wait(barrier, seqs - 1 + groups - 1)

    def push_copy(sender, to):
        return pltpu.make_async_remote_copy(
            src_ref=push.at[:, to * part : (to + 1) * part, :],
            dst_ref=gath.at[sender],
            send_sem=push_s.at[to],
            recv_sem=push_r.at[sender],
            device_id=(o * inner + to, hd),
            device_id_type=MESH,
        )

    def dec_copy(sender, to):
        return pltpu.make_async_remote_copy(
            src_ref=dec,
            dst_ref=dgath.at[sender],
            send_sem=dec_s.at[to],
            recv_sem=dec_r.at[sender],
            device_id=(o * inner + to, hd),
            device_id_type=MESH,
        )

    for j in range(inner):

        @pl.when(j != i)
        def _(j=j):
            push_copy(i, j).start()
            dec_copy(i, j).start()

    gath[i] = push[:, pl.ds(pl.multiple_of(i * part, part), part), :]
    dgath[i] = dec[...]

    loads[3].wait()
    loads[4].wait()
    loads[5].wait()
    total = c[...]
    middle = total[tokens // 2 - 1 : tokens // 2]
    last = total[tokens - 1 : tokens]
    down = k[...].astype(F32) * jnp.exp(middle - total)
    kdn[...] = down.astype(BF16)
    scale[...] = jnp.exp(last - total)
    ktail[...] = down * jnp.exp(last - middle)
    scores = []
    for h in range(heads):
        at = cols[h]
        g_h = g[:, at]
        score = jnp.where(lower, product(g_h, v[:, at], 1, 1), 0.0).astype(BF16)
        scores.append(score)
        total = c[:, at]
        middle = total[tokens // 2 - 1 : tokens // 2]
        from_start = product(twice(g_h, 1), both(s[h], 1), 1, 1) * jnp.exp(total)
        kdn_h = kdn[:, at]
        qup_h = qup[:, at]
        inside = product(score, kdn_h, 1, 0)
        back = product(score, qup_h, 0, 0)
        gq_out[:, at] = (jnp.exp(total - middle) * inside + from_start).astype(BF16)
        gk_part[:, at] = jnp.exp(middle - total) * back
        terms[:, at] = (
            qup_h.astype(F32) * inside - kdn_h.astype(F32) * back + q[:, at].astype(F32) * from_start
        )

    for j in range(inner):

        @pl.when(j != i)
        def _(j=j):
            push_copy(j, j).wait_recv()
            dec_copy(j, j).wait_recv()

    for h in range(heads):
        state = gath[inner - 1, h].astype(F32)
        decay = dgath[inner - 1, h : h + 1]
        for j in range(inner - 2, -1, -1):
            alone[j, h] = state
            decays[j, h] = jnp.broadcast_to(decay, (8, LANES))
            step = dgath[j, h : h + 1]
            state = gath[j, h].astype(F32) + step * state
            decay = decay * step
        alone[inner - 1, h] = state
        decays[inner - 1, h] = jnp.broadcast_to(decay, (8, LANES))

    def hop_copy():
        return pltpu.make_async_remote_copy(
            src_ref=leave,
            dst_ref=carry,
            send_sem=hop_s,
            recv_sem=hop_r,
            device_id=(p - inner, hd),
            device_id_type=MESH,
        )

    share = pl.ds(pl.multiple_of(i * part, part), part)

    def end_copy(sender, to, where):
        return pltpu.make_async_remote_copy(
            src_ref=ends.at[to],
            dst_ref=incoming.at[:, where, :],
            send_sem=end_s.at[to],
            recv_sem=end_r.at[sender],
            device_id=(o * inner + to, hd),
            device_id_type=MESH,
        )

    def hand_back():
        for h in range(heads):
            from_later = carry[h].astype(F32)
            ends[inner - 1, h] = carry[h]
            for j in range(inner - 1):
                ends[j, h] = (alone[j, h] + decays[j, h, 0:1] * from_later).astype(BF16)
        for j in range(inner):

            @pl.when(j != i)
            def _(j=j):
                end_copy(i, j, share).start()

        incoming[:, share, :] = ends[i]

    def pass_on():
        for h in range(heads):
            leave[h] = (
                alone[inner - 1, h] + decays[inner - 1, h, 0:1] * carry[h].astype(F32)
            ).astype(BF16)
        hop_copy().start()

    @pl.when(o == outer - 1)
    def _():
        carry[...] = jnp.zeros_like(carry)
        if outer > 1:
            pass_on()
        hand_back()

    for h in range(heads):
        at = cols[h]
        total = c[:, at]
        middle = total[tokens // 2 - 1 : tokens // 2]
        k_high, k_low = halves(k[:, at].astype(F32) * jnp.exp(middle - total))
        q_high, q_low = halves(q[:, at].astype(F32) * jnp.exp(total - middle))
        weight = product(
            jnp.concatenate([k_high, k_high], axis=1), jnp.concatenate([q_high, q_low], axis=1), 1, 1
        ) + product(k_low, q_high, 1, 1)
        weight = jnp.where(upper, weight, 0.0)
        gv_part[:, at] = product(both(weight, 1), twice(g[:, at], 0), 1, 0)
    gg_part[...] = product(twice(upper_b, 1), both(terms[...], 0), 1, 0)

    if outer > 1:

        @pl.when(o < outer - 1)
        def _():
            hop_copy().wait_recv()

            @pl.when(o > 0)
            def _():
                pass_on()

            hand_back()

    for h in range(heads):
        turned[h] = s[h].T
        at = cols[h]
        tail_high, tail_low = halves(ktail[:, at])
        tails[h, :, 0:LANES] = tail_high
        tails[h, :, LANES:] = tail_low

    for j in range(inner):

        @pl.when(j != i)
        def _(j=j):
            end_copy(j, j, slice(j * part, (j + 1) * part)).wait_recv()

    for h in range(heads):
        at = cols[h]
        gv[0:tokens, at] = (
            gv_part[:, at] + product(tails[h], twice(incoming[h], 1), 1, 1)
        ).astype(BF16)

    def edge_copy():
        return pltpu.make_async_remote_copy(
            src_ref=gv.at[0:EDGE],
            dst_ref=gv.at[tokens : tokens + EDGE],
            send_sem=edge_s,
            recv_sem=edge_r,
            device_id=(p - 1, hd),
            device_id_type=MESH,
        )

    @pl.when(p > 0)
    def _():
        edge_copy().start()

    @pl.when(p == seqs - 1)
    def _():
        gv[tokens : tokens + EDGE] = jnp.zeros((EDGE, columns), BF16)

    loads[6].wait()
    loads[7].wait()

    def convolve(first, end):
        rows = gv[first : end + EDGE].astype(F32)
        result = w[0:1] * rows[: end - first]
        for tap in range(1, taps):
            result = result + w[tap : tap + 1] * rows[tap : tap + end - first]
        gi[first:end] = result.astype(BF16)

    def row_copy(sender, to):
        return pltpu.make_async_remote_copy(
            src_ref=gi.at[to * own_rows : (to + 1) * own_rows],
            dst_ref=gi_out.at[:, pl.ds(pl.multiple_of(sender * columns, LANES), columns)],
            send_sem=row_s.at[to],
            recv_sem=row_r.at[sender],
            device_id=(p, to),
            device_id_type=MESH,
        )

    def keep_copy(to):
        return pltpu.make_async_copy(
            gi.at[to * own_rows : (to + 1) * own_rows], gi_out.at[:, mine], row_s.at[to]
        )

    def hand_out(to):
        @pl.when(to != hd)
        def _():
            row_copy(hd, to).start()

        @pl.when(to == hd)
        def _():
            keep_copy(to).start()

    for to in range(groups - 1):
        convolve(to * own_rows, (to + 1) * own_rows)
        hand_out(to)

    for h in range(heads):
        at = cols[h]
        later = product(v[:, at], incoming[h], 1, 0)
        gk_out[:, at] = (gk_part[:, at] + scale[:, at] * later).astype(BF16)
        own = jnp.sum(incoming[h].astype(F32) * turned[h], axis=0, keepdims=True)
        gg = (
            gg_part[:, at]
            + product(strict_b, (ktail[:, at] * later).astype(BF16), 1, 0)
            + own * dec[h : h + 1]
        )
        gg_out[:, at] = gg.astype(BF16)

    @pl.when(p < seqs - 1)
    def _():
        edge_copy().wait_recv()

    convolve((groups - 1) * own_rows, tokens)
    hand_out(groups - 1)

    rows = gv[...].astype(F32)
    x_f = x[...].astype(F32)
    for tap in range(taps):
        sums[tap : tap + 1] = jnp.sum(x_f * rows[tap : tap + tokens], axis=0, keepdims=True)

    def sum_copy(sender, to):
        return pltpu.make_async_remote_copy(
            src_ref=sums,
            dst_ref=all_sums.at[sender],
            send_sem=sum_s.at[to],
            recv_sem=sum_r.at[sender],
            device_id=(to, hd),
            device_id_type=MESH,
        )

    def send_sum(n, carried):
        sum_copy(p, lax.rem(p + n, seqs)).start()
        return carried

    lax.fori_loop(1, seqs, send_sum, 0)
    all_sums[p] = sums[...]

    def take_sum(n, carried):
        other = lax.rem(p + n, seqs)
        sum_copy(other, other).wait_recv()
        return carried

    lax.fori_loop(1, seqs, take_sum, 0)
    added = lax.fori_loop(
        0, seqs, lambda n, value: value + all_sums[n], jnp.zeros((taps, columns), F32)
    )
    gw_out[...] = added

    for sender in range(groups):

        @pl.when(sender != hd)
        def _(sender=sender):
            row_copy(sender, sender).wait_recv()

    for to in range(groups):

        @pl.when(to != hd)
        def _(to=to):
            row_copy(hd, to).wait_send()

        @pl.when(to == hd)
        def _(to=to):
            keep_copy(to).wait()

    def sent_sum(n, carried):
        sum_copy(p, lax.rem(p + n, seqs)).wait_send()
        return carried

    lax.fori_loop(1, seqs, sent_sum, 0)
    for j in range(inner):

        @pl.when(j != i)
        def _(j=j):
            push_copy(i, j).wait_send()
            dec_copy(i, j).wait_send()
            end_copy(i, j, share).wait_send()

    if outer > 1:

        @pl.when(o > 0)
        def _():
            hop_copy().wait_send()

    @pl.when(p > 0)
    def _():
        edge_copy().wait_send()


def deliver(*refs):
    count = len(refs) // 2
    copies = [
        pltpu.make_async_copy(refs[n], refs[count + n], refs[-1].at[n]) for n in range(count)
    ]
    for copy in copies:
        copy.start()
    for copy in copies:
        copy.wait()


def solution(mesh):
    seqs, groups = mesh.shape["seq"], mesh.shape["head"]
    inner = 4 if seqs % 4 == 0 else 1

    def per_device(queries, key_rows, values, conv_input, log_gates, grad_output, saved_state, conv_kernel):
        tokens, columns = queries.shape
        heads = saved_state.shape[1]
        taps = conv_kernel.shape[0]
        part = LANES // inner
        flat = (tokens, columns)
        dma = pltpu.SemaphoreType.DMA
        vmem = pltpu.VMEM
        shapes = (
            jax.ShapeDtypeStruct(flat, BF16),
            jax.ShapeDtypeStruct(flat, BF16),
            jax.ShapeDtypeStruct(flat, BF16),
            jax.ShapeDtypeStruct((tokens // groups, columns * groups), BF16),
            jax.ShapeDtypeStruct((taps, columns), F32),
        )
        results = pl.pallas_call(
            functools.partial(body, seqs, groups, inner, heads, tokens, taps),
            out_shape=tuple(vmem(made.shape, made.dtype) for made in shapes),
            in_specs=[pl.BlockSpec(memory_space=pltpu.HBM)] * 8,
            out_specs=[pl.BlockSpec(memory_space=pltpu.VMEM)] * 5,
            scratch_shapes=[vmem(flat, BF16)] * 6
            + [
                vmem((heads, LANES, LANES), F32),
                vmem((taps, columns), F32),
                vmem((heads, LANES, LANES), F32),
                vmem((heads, tokens, 2 * LANES), BF16),
                vmem(flat, F32),
                vmem(flat, BF16),
                vmem(flat, BF16),
                vmem(flat, F32),
                vmem(flat, F32),
                vmem(flat, F32),
                vmem(flat, F32),
                vmem(flat, F32),
                vmem(flat, F32),
                vmem((heads, LANES, LANES), BF16),
                vmem((heads, LANES), F32),
                vmem((inner, heads, part, LANES), BF16),
                vmem((inner, heads, LANES), F32),
                vmem((inner, heads, part, LANES), F32),
                vmem((inner, heads, 8, LANES), F32),
                vmem((heads, part, LANES), BF16),
                vmem((heads, part, LANES), BF16),
                vmem((inner, heads, part, LANES), BF16),
                vmem((heads, LANES, LANES), BF16),
                vmem((tokens + EDGE, columns), BF16),
                vmem(flat, BF16),
                vmem((taps, columns), F32),
                vmem((seqs, taps, columns), F32),
                dma((8,)),
                dma((inner,)),
                dma((inner,)),
                dma((inner,)),
                dma((inner,)),
                dma,
                dma,
                dma((inner,)),
                dma((inner,)),
                dma,
                dma,
                dma((groups,)),
                dma((groups,)),
                dma((seqs,)),
                dma((seqs,)),
            ],
            compiler_params=pltpu.CompilerParams(
                collective_id=0, has_side_effects=True, vmem_limit_bytes=60 * 1024 * 1024
            ),
        )(queries, key_rows, values, conv_input, log_gates, grad_output, saved_state, conv_kernel)
        return pl.pallas_call(
            deliver,
            out_shape=shapes,
            in_specs=[pl.BlockSpec(memory_space=pl.ANY)] * len(shapes),
            out_specs=[pl.BlockSpec(memory_space=pltpu.HBM)] * len(shapes),
            scratch_shapes=[dma((len(shapes),))],
        )(*results)

    return jax.shard_map(
        per_device,
        mesh=mesh,
        in_specs=(
            P("seq", "head"),
            P("seq", "head"),
            P("seq", "head"),
            P("seq", "head"),
            P("seq", "head"),
            P("seq", "head"),
            P("seq", "head", None, None),
            P(),
        ),
        out_specs=(
            P("seq", "head"),
            P("seq", "head"),
            P("seq", "head"),
            P(("seq", "head"), None),
            P(None, "head"),
        ),
        check_vma=False,
    )
```

```python
import functools

import jax
import jax.numpy as jnp
from jax import lax
from jax.experimental import pallas as pl
from jax.experimental.pallas import tpu as pltpu
from jax.sharding import PartitionSpec as P

MESH = pl.DeviceIdType.MESH
F32 = jnp.float32
BF16 = jnp.bfloat16
LANES = 128
EDGE = 16


def product(a, b, dim_a, dim_b):
    return lax.dot_general(
        a, b, (((dim_a,), (dim_b,)), ((), ())), preferred_element_type=F32
    )


def halves(x):
    high = x.astype(BF16)
    return high, (x - high.astype(F32)).astype(BF16)


def both(x, axis):
    return jnp.concatenate(halves(x), axis=axis)


def twice(x, axis):
    return jnp.concatenate([x, x], axis=axis)


def body(
    seqs, groups, inner, heads, tokens, taps,
    q_in, k_in, v_in, x_in, l_in, g_in, s_in, w_in,
    gq_out, gk_out, gg_out, gi_out, gw_out,
    q, k, v, x, l, g, s, w,
    turned, tails, c, qup, kdn, scale, ktail, terms, gk_part, gv_part, gg_part,
    push, dec, gath, dgath, alone, decays, carry, leave, ends, incoming,
    gv, gi, sums, all_sums,
    in_sem, push_s, push_r, dec_s, dec_r, hop_s, hop_r, end_s, end_r,
    edge_s, edge_r, row_s, row_r, sum_s, sum_r,
):
    p = lax.axis_index("seq")
    hd = lax.axis_index("head")
    o, i = p // inner, p % inner
    outer = seqs // inner
    part = LANES // inner
    columns = heads * LANES
    own_rows = tokens // groups
    cols = [slice(h * LANES, (h + 1) * LANES) for h in range(heads)]

    mine = pl.ds(pl.multiple_of(hd * columns, LANES), columns)
    loads = [
        pltpu.make_async_copy(src, dst, in_sem.at[n])
        for n, (src, dst) in enumerate(
            [(l_in, l), (q_in, q), (g_in, g), (k_in, k), (v_in, v), (s_in.at[0], s), (x_in, x), (w_in.at[:, mine], w)]
        )
    ]
    for load in loads:
        load.start()

    def greet(n, carried):
        pl.semaphore_signal(
            barrier, inc=1, device_id=(lax.rem(p + n, seqs), hd), device_id_type=MESH
        )
        return carried

    barrier = pltpu.get_barrier_semaphore()
    lax.fori_loop(1, seqs, greet, 0)
    for n in range(1, groups):
        pl.semaphore_signal(
            barrier, inc=1, device_id=(p, lax.rem(hd + n, groups)), device_id_type=MESH
        )

    row = lax.broadcasted_iota(jnp.int32, (tokens, tokens), 0)
    col = lax.broadcasted_iota(jnp.int32, (tokens, tokens), 1)
    lower = row >= col
    upper = col >= row
    lower_b = jnp.where(lower, 1.0, 0.0).astype(BF16)
    upper_b = jnp.where(upper, 1.0, 0.0).astype(BF16)
    strict_b = jnp.where(row > col, 1.0, 0.0).astype(BF16)

    loads[0].wait()
    total = product(lower_b, l[...], 1, 0)
    c[...] = total
    middle = total[tokens // 2 - 1 : tokens // 2]
    last = total[tokens - 1 : tokens]
    to_middle = jnp.exp(middle)
    grow = jnp.exp(total - middle)
    whole = jnp.exp(last)
    for h in range(heads):
        dec[h : h + 1] = whole[:, cols[h]]
    loads[1].wait()
    up = q[...].astype(F32) * grow
    qup[...] = up.astype(BF16)
    full = up * to_middle
    loads[2].wait()
    for h in range(heads):
        push[h] = product(twice(g[:, cols[h]], 0), both(full[:, cols[h]], 0), 0, 0).astype(BF16)

    pl.semaphore_wait(barrier, seqs - 1 + groups - 1)

    def push_copy(sender, to):
        return pltpu.make_async_remote_copy(
            src_ref=push.at[:, to * part : (to + 1) * part, :],
            dst_ref=gath.at[sender],
            send_sem=push_s.at[to],
            recv_sem=push_r.at[sender],
            device_id=(o * inner + to, hd),
            device_id_type=MESH,
        )

    def dec_copy(sender, to):
        return pltpu.make_async_remote_copy(
            src_ref=dec,
            dst_ref=dgath.at[sender],
            send_sem=dec_s.at[to],
            recv_sem=dec_r.at[sender],
            device_id=(o * inner + to, hd),
            device_id_type=MESH,
        )

    for j in range(inner):

        @pl.when(j != i)
        def _(j=j):
            push_copy(i, j).start()
            dec_copy(i, j).start()

    gath[i] = push[:, pl.ds(pl.multiple_of(i * part, part), part), :]
    dgath[i] = dec[...]

    loads[3].wait()
    loads[4].wait()
    loads[5].wait()
    total = c[...]
    middle = total[tokens // 2 - 1 : tokens // 2]
    last = total[tokens - 1 : tokens]
    down = k[...].astype(F32) * jnp.exp(middle - total)
    kdn[...] = down.astype(BF16)
    scale[...] = jnp.exp(last - total)
    ktail[...] = down * jnp.exp(last - middle)
    scores = []
    for h in range(heads):
        at = cols[h]
        g_h = g[:, at]
        score = jnp.where(lower, product(g_h, v[:, at], 1, 1), 0.0).astype(BF16)
        scores.append(score)
        total = c[:, at]
        middle = total[tokens // 2 - 1 : tokens // 2]
        from_start = product(twice(g_h, 1), both(s[h], 1), 1, 1) * jnp.exp(total)
        kdn_h = kdn[:, at]
        qup_h = qup[:, at]
        inside = product(score, kdn_h, 1, 0)
        back = product(score, qup_h, 0, 0)
        gq_out[:, at] = (jnp.exp(total - middle) * inside + from_start).astype(BF16)
        gk_part[:, at] = jnp.exp(middle - total) * back
        terms[:, at] = (
            qup_h.astype(F32) * inside - kdn_h.astype(F32) * back + q[:, at].astype(F32) * from_start
        )

    for j in range(inner):

        @pl.when(j != i)
        def _(j=j):
            push_copy(j, j).wait_recv()
            dec_copy(j, j).wait_recv()

    for h in range(heads):
        state = gath[inner - 1, h].astype(F32)
        decay = dgath[inner - 1, h : h + 1]
        for j in range(inner - 2, -1, -1):
            alone[j, h] = state
            decays[j, h] = jnp.broadcast_to(decay, (8, LANES))
            step = dgath[j, h : h + 1]
            state = gath[j, h].astype(F32) + step * state
            decay = decay * step
        alone[inner - 1, h] = state
        decays[inner - 1, h] = jnp.broadcast_to(decay, (8, LANES))

    def hop_copy():
        return pltpu.make_async_remote_copy(
            src_ref=leave,
            dst_ref=carry,
            send_sem=hop_s,
            recv_sem=hop_r,
            device_id=(p - inner, hd),
            device_id_type=MESH,
        )

    share = pl.ds(pl.multiple_of(i * part, part), part)

    def end_copy(sender, to, where):
        return pltpu.make_async_remote_copy(
            src_ref=ends.at[to],
            dst_ref=incoming.at[:, where, :],
            send_sem=end_s.at[to],
            recv_sem=end_r.at[sender],
            device_id=(o * inner + to, hd),
            device_id_type=MESH,
        )

    def hand_back():
        for h in range(heads):
            from_later = carry[h].astype(F32)
            ends[inner - 1, h] = carry[h]
            for j in range(inner - 1):
                ends[j, h] = (alone[j, h] + decays[j, h, 0:1] * from_later).astype(BF16)
        for j in range(inner):

            @pl.when(j != i)
            def _(j=j):
                end_copy(i, j, share).start()

        incoming[:, share, :] = ends[i]

    def pass_on():
        for h in range(heads):
            leave[h] = (
                alone[inner - 1, h] + decays[inner - 1, h, 0:1] * carry[h].astype(F32)
            ).astype(BF16)
        hop_copy().start()

    @pl.when(o == outer - 1)
    def _():
        carry[...] = jnp.zeros_like(carry)
        if outer > 1:
            pass_on()
        hand_back()

    for h in range(heads):
        at = cols[h]
        total = c[:, at]
        middle = total[tokens // 2 - 1 : tokens // 2]
        k_high, k_low = halves(k[:, at].astype(F32) * jnp.exp(middle - total))
        q_high, q_low = halves(q[:, at].astype(F32) * jnp.exp(total - middle))
        weight = product(
            jnp.concatenate([k_high, k_high], axis=1), jnp.concatenate([q_high, q_low], axis=1), 1, 1
        ) + product(k_low, q_high, 1, 1)
        weight = jnp.where(upper, weight, 0.0)
        gv_part[:, at] = product(both(weight, 1), twice(g[:, at], 0), 1, 0)
    gg_part[...] = product(twice(upper_b, 1), both(terms[...], 0), 1, 0)

    if outer > 1:

        @pl.when(o < outer - 1)
        def _():
            hop_copy().wait_recv()

            @pl.when(o > 0)
            def _():
                pass_on()

            hand_back()

    for h in range(heads):
        turned[h] = s[h].T
        at = cols[h]
        tail_high, tail_low = halves(ktail[:, at])
        tails[h, :, 0:LANES] = tail_high
        tails[h, :, LANES:] = tail_low

    for j in range(inner):

        @pl.when(j != i)
        def _(j=j):
            end_copy(j, j, slice(j * part, (j + 1) * part)).wait_recv()

    for h in range(heads):
        at = cols[h]
        gv[0:tokens, at] = (
            gv_part[:, at] + product(tails[h], twice(incoming[h], 1), 1, 1)
        ).astype(BF16)

    def edge_copy():
        return pltpu.make_async_remote_copy(
            src_ref=gv.at[0:EDGE],
            dst_ref=gv.at[tokens : tokens + EDGE],
            send_sem=edge_s,
            recv_sem=edge_r,
            device_id=(p - 1, hd),
            device_id_type=MESH,
        )

    @pl.when(p > 0)
    def _():
        edge_copy().start()

    @pl.when(p == seqs - 1)
    def _():
        gv[tokens : tokens + EDGE] = jnp.zeros((EDGE, columns), BF16)

    loads[6].wait()
    loads[7].wait()

    def convolve(first, end):
        rows = gv[first : end + EDGE].astype(F32)
        result = w[0:1] * rows[: end - first]
        for tap in range(1, taps):
            result = result + w[tap : tap + 1] * rows[tap : tap + end - first]
        gi[first:end] = result.astype(BF16)

    def row_copy(sender, to):
        return pltpu.make_async_remote_copy(
            src_ref=gi.at[to * own_rows : (to + 1) * own_rows],
            dst_ref=gi_out.at[:, pl.ds(pl.multiple_of(sender * columns, LANES), columns)],
            send_sem=row_s.at[to],
            recv_sem=row_r.at[sender],
            device_id=(p, to),
            device_id_type=MESH,
        )

    def keep_copy(to):
        return pltpu.make_async_copy(
            gi.at[to * own_rows : (to + 1) * own_rows], gi_out.at[:, mine], row_s.at[to]
        )

    def hand_out(to):
        @pl.when(to != hd)
        def _():
            row_copy(hd, to).start()

        @pl.when(to == hd)
        def _():
            keep_copy(to).start()

    for to in range(groups - 1):
        convolve(to * own_rows, (to + 1) * own_rows)
        hand_out(to)

    for h in range(heads):
        at = cols[h]
        later = product(v[:, at], incoming[h], 1, 0)
        gk_out[:, at] = (gk_part[:, at] + scale[:, at] * later).astype(BF16)
        own = jnp.sum(incoming[h].astype(F32) * turned[h], axis=0, keepdims=True)
        gg = (
            gg_part[:, at]
            + product(strict_b, (ktail[:, at] * later).astype(BF16), 1, 0)
            + own * dec[h : h + 1]
        )
        gg_out[:, at] = gg.astype(BF16)

    @pl.when(p < seqs - 1)
    def _():
        edge_copy().wait_recv()

    convolve((groups - 1) * own_rows, tokens)
    hand_out(groups - 1)

    rows = gv[...].astype(F32)
    x_f = x[...].astype(F32)
    for tap in range(taps):
        sums[tap : tap + 1] = jnp.sum(x_f * rows[tap : tap + tokens], axis=0, keepdims=True)

    def sum_copy(sender, to):
        return pltpu.make_async_remote_copy(
            src_ref=sums,
            dst_ref=all_sums.at[sender],
            send_sem=sum_s.at[to],
            recv_sem=sum_r.at[sender],
            device_id=(to, hd),
            device_id_type=MESH,
        )

    def send_sum(n, carried):
        sum_copy(p, lax.rem(p + n, seqs)).start()
        return carried

    lax.fori_loop(1, seqs, send_sum, 0)
    all_sums[p] = sums[...]

    def take_sum(n, carried):
        other = lax.rem(p + n, seqs)
        sum_copy(other, other).wait_recv()
        return carried

    lax.fori_loop(1, seqs, take_sum, 0)
    added = lax.fori_loop(
        0, seqs, lambda n, value: value + all_sums[n], jnp.zeros((taps, columns), F32)
    )
    gw_out[...] = added

    for sender in range(groups):

        @pl.when(sender != hd)
        def _(sender=sender):
            row_copy(sender, sender).wait_recv()

    for to in range(groups):

        @pl.when(to != hd)
        def _(to=to):
            row_copy(hd, to).wait_send()

        @pl.when(to == hd)
        def _(to=to):
            keep_copy(to).wait()

    def sent_sum(n, carried):
        sum_copy(p, lax.rem(p + n, seqs)).wait_send()
        return carried

    lax.fori_loop(1, seqs, sent_sum, 0)
    for j in range(inner):

        @pl.when(j != i)
        def _(j=j):
            push_copy(i, j).wait_send()
            dec_copy(i, j).wait_send()
            end_copy(i, j, share).wait_send()

    if outer > 1:

        @pl.when(o > 0)
        def _():
            hop_copy().wait_send()

    @pl.when(p > 0)
    def _():
        edge_copy().wait_send()


def deliver(*refs):
    count = len(refs) // 2
    copies = [
        pltpu.make_async_copy(refs[n], refs[count + n], refs[-1].at[n]) for n in range(count)
    ]
    for copy in copies:
        copy.start()
    for copy in copies:
        copy.wait()


def solution(mesh):
    seqs, groups = mesh.shape["seq"], mesh.shape["head"]
    inner = 4 if seqs % 4 == 0 else 1

    def per_device(queries, key_rows, values, conv_input, log_gates, grad_output, saved_state, conv_kernel):
        tokens, columns = queries.shape
        heads = saved_state.shape[1]
        taps = conv_kernel.shape[0]
        part = LANES // inner
        flat = (tokens, columns)
        dma = pltpu.SemaphoreType.DMA
        vmem = pltpu.VMEM
        shapes = (
            jax.ShapeDtypeStruct(flat, BF16),
            jax.ShapeDtypeStruct(flat, BF16),
            jax.ShapeDtypeStruct(flat, BF16),
            jax.ShapeDtypeStruct((tokens // groups, columns * groups), BF16),
            jax.ShapeDtypeStruct((taps, columns), F32),
        )
        results = pl.pallas_call(
            functools.partial(body, seqs, groups, inner, heads, tokens, taps),
            out_shape=tuple(vmem(made.shape, made.dtype) for made in shapes),
            in_specs=[pl.BlockSpec(memory_space=pltpu.HBM)] * 8,
            out_specs=[pl.BlockSpec(memory_space=pltpu.VMEM)] * 5,
            scratch_shapes=[vmem(flat, BF16)] * 6
            + [
                vmem((heads, LANES, LANES), F32),
                vmem((taps, columns), F32),
                vmem((heads, LANES, LANES), F32),
                vmem((heads, tokens, 2 * LANES), BF16),
                vmem(flat, F32),
                vmem(flat, BF16),
                vmem(flat, BF16),
                vmem(flat, F32),
                vmem(flat, F32),
                vmem(flat, F32),
                vmem(flat, F32),
                vmem(flat, F32),
                vmem(flat, F32),
                vmem((heads, LANES, LANES), BF16),
                vmem((heads, LANES), F32),
                vmem((inner, heads, part, LANES), BF16),
                vmem((inner, heads, LANES), F32),
                vmem((inner, heads, part, LANES), F32),
                vmem((inner, heads, 8, LANES), F32),
                vmem((heads, part, LANES), BF16),
                vmem((heads, part, LANES), BF16),
                vmem((inner, heads, part, LANES), BF16),
                vmem((heads, LANES, LANES), BF16),
                vmem((tokens + EDGE, columns), BF16),
                vmem(flat, BF16),
                vmem((taps, columns), F32),
                vmem((seqs, taps, columns), F32),
                dma((8,)),
                dma((inner,)),
                dma((inner,)),
                dma((inner,)),
                dma((inner,)),
                dma,
                dma,
                dma((inner,)),
                dma((inner,)),
                dma,
                dma,
                dma((groups,)),
                dma((groups,)),
                dma((seqs,)),
                dma((seqs,)),
            ],
            compiler_params=pltpu.CompilerParams(
                collective_id=0, has_side_effects=True, vmem_limit_bytes=60 * 1024 * 1024
            ),
        )(queries, key_rows, values, conv_input, log_gates, grad_output, saved_state, conv_kernel)
        return pl.pallas_call(
            deliver,
            out_shape=shapes,
            in_specs=[pl.BlockSpec(memory_space=pltpu.VMEM)] * len(shapes),
            out_specs=[pl.BlockSpec(memory_space=pltpu.HBM)] * len(shapes),
            scratch_shapes=[dma((len(shapes),))],
        )(*results)

    return jax.shard_map(
        per_device,
        mesh=mesh,
        in_specs=(
            P("seq", "head"),
            P("seq", "head"),
            P("seq", "head"),
            P("seq", "head"),
            P("seq", "head"),
            P("seq", "head"),
            P("seq", "head", None, None),
            P(),
        ),
        out_specs=(
            P("seq", "head"),
            P("seq", "head"),
            P("seq", "head"),
            P(("seq", "head"), None),
            P(None, "head"),
        ),
        check_vma=False,
    )
```

```python
import functools

import jax
import jax.numpy as jnp
from jax import lax
from jax.experimental import pallas as pl
from jax.experimental.pallas import tpu as pltpu
from jax.sharding import PartitionSpec as P

MESH = pl.DeviceIdType.MESH
F32 = jnp.float32
BF16 = jnp.bfloat16
LANES = 128
EDGE = 16


def product(a, b, dim_a, dim_b):
    return lax.dot_general(
        a, b, (((dim_a,), (dim_b,)), ((), ())), preferred_element_type=F32
    )


def halves(x):
    high = x.astype(BF16)
    return high, (x - high.astype(F32)).astype(BF16)


def both(x, axis):
    return jnp.concatenate(halves(x), axis=axis)


def twice(x, axis):
    return jnp.concatenate([x, x], axis=axis)


def body(
    seqs, groups, inner, heads, tokens, taps,
    q_in, k_in, v_in, x_in, l_in, g_in, s_in, w_in,
    gq_out, gk_out, gg_out, gi_out, gw_out,
    q, k, v, x, l, g, s, w,
    turned, tails, c, qup, kdn, scale, ktail, terms, gk_part, gv_part, gg_part,
    push, dec, gath, dgath, alone, decays, carry, leave, ends, incoming,
    gv, gi, sums, all_sums,
    in_sem, push_s, push_r, dec_s, dec_r, hop_s, hop_r, end_s, end_r,
    before_s, before_r, edge_s, edge_r, row_s, row_r, sum_s, sum_r,
):
    p = lax.axis_index("seq")
    hd = lax.axis_index("head")
    o, i = p // inner, p % inner
    outer = seqs // inner
    part = LANES // inner
    columns = heads * LANES
    own_rows = tokens // groups
    half = heads // 2
    chunks = [(0, half), (half, heads)] if half else [(0, heads)]
    cols = [slice(h * LANES, (h + 1) * LANES) for h in range(heads)]

    mine = pl.ds(pl.multiple_of(hd * columns, LANES), columns)
    loads = [
        pltpu.make_async_copy(src, dst, in_sem.at[n])
        for n, (src, dst) in enumerate(
            [(l_in, l), (q_in, q), (g_in, g), (k_in, k), (v_in, v), (s_in.at[0], s), (x_in, x.at[EDGE:]), (w_in.at[:, mine], w)]
        )
    ]
    for load in loads:
        load.start()

    def greet(n, carried):
        pl.semaphore_signal(
            barrier, inc=1, device_id=(lax.rem(p + n, seqs), hd), device_id_type=MESH
        )
        return carried

    barrier = pltpu.get_barrier_semaphore()
    lax.fori_loop(1, seqs, greet, 0)
    for n in range(1, groups):
        pl.semaphore_signal(
            barrier, inc=1, device_id=(p, lax.rem(hd + n, groups)), device_id_type=MESH
        )

    row = lax.broadcasted_iota(jnp.int32, (tokens, tokens), 0)
    col = lax.broadcasted_iota(jnp.int32, (tokens, tokens), 1)
    lower = row >= col
    upper = col >= row
    lower_b = jnp.where(lower, 1.0, 0.0).astype(BF16)
    upper_b = jnp.where(upper, 1.0, 0.0).astype(BF16)
    strict_b = jnp.where(row > col, 1.0, 0.0).astype(BF16)

    loads[0].wait()
    total = product(lower_b, l[...], 1, 0)
    c[...] = total
    middle = total[tokens // 2 - 1 : tokens // 2]
    last = total[tokens - 1 : tokens]
    to_middle = jnp.exp(middle)
    grow = jnp.exp(total - middle)
    whole = jnp.exp(last)
    for h in range(heads):
        dec[h : h + 1] = whole[:, cols[h]]
    loads[1].wait()
    up = q[...].astype(F32) * grow
    qup[...] = up.astype(BF16)
    full = up * to_middle
    loads[2].wait()

    def push_copy(n, sender, to):
        first, end = chunks[n]
        return pltpu.make_async_remote_copy(
            src_ref=push.at[first:end, to * part : (to + 1) * part, :],
            dst_ref=gath.at[sender, first:end],
            send_sem=push_s.at[n, to],
            recv_sem=push_r.at[n, sender],
            device_id=(o * inner + to, hd),
            device_id_type=MESH,
        )

    def dec_copy(sender, to):
        return pltpu.make_async_remote_copy(
            src_ref=dec,
            dst_ref=dgath.at[sender],
            send_sem=dec_s.at[to],
            recv_sem=dec_r.at[sender],
            device_id=(o * inner + to, hd),
            device_id_type=MESH,
        )

    def before_copy():
        return pltpu.make_async_remote_copy(
            src_ref=x.at[tokens : tokens + EDGE],
            dst_ref=x.at[0:EDGE],
            send_sem=before_s,
            recv_sem=before_r,
            device_id=(p + 1, hd),
            device_id_type=MESH,
        )

    for n, (first, end) in enumerate(chunks):
        for h in range(first, end):
            push[h] = product(
                twice(g[:, cols[h]], 0), both(full[:, cols[h]], 0), 0, 0
            ).astype(BF16)
        if n == 0:
            pl.semaphore_wait(barrier, seqs - 1 + groups - 1)
        for j in range(inner):

            @pl.when(j != i)
            def _(j=j):
                if n == 0:
                    dec_copy(i, j).start()
                push_copy(n, i, j).start()

    loads[6].wait()

    @pl.when(p < seqs - 1)
    def _():
        before_copy().start()

    @pl.when(p == 0)
    def _():
        x[0:EDGE] = jnp.zeros((EDGE, columns), BF16)

    gath[i] = push[:, pl.ds(pl.multiple_of(i * part, part), part), :]
    dgath[i] = dec[...]

    loads[3].wait()
    loads[4].wait()
    loads[5].wait()
    total = c[...]
    middle = total[tokens // 2 - 1 : tokens // 2]
    last = total[tokens - 1 : tokens]
    down = k[...].astype(F32) * jnp.exp(middle - total)
    kdn[...] = down.astype(BF16)
    scale[...] = jnp.exp(last - total)
    ktail[...] = down * jnp.exp(last - middle)
    scores = []
    for h in range(heads):
        at = cols[h]
        g_h = g[:, at]
        score = jnp.where(lower, product(g_h, v[:, at], 1, 1), 0.0).astype(BF16)
        scores.append(score)
        total = c[:, at]
        middle = total[tokens // 2 - 1 : tokens // 2]
        from_start = product(twice(g_h, 1), both(s[h], 1), 1, 1) * jnp.exp(total)
        kdn_h = kdn[:, at]
        qup_h = qup[:, at]
        inside = product(score, kdn_h, 1, 0)
        back = product(score, qup_h, 0, 0)
        gq_out[:, at] = (jnp.exp(total - middle) * inside + from_start).astype(BF16)
        gk_part[:, at] = jnp.exp(middle - total) * back
        terms[:, at] = (
            qup_h.astype(F32) * inside - kdn_h.astype(F32) * back + q[:, at].astype(F32) * from_start
        )

    share = pl.ds(pl.multiple_of(i * part, part), part)

    def hop_copy(n):
        first, end = chunks[n]
        return pltpu.make_async_remote_copy(
            src_ref=leave.at[first:end],
            dst_ref=carry.at[first:end],
            send_sem=hop_s.at[n],
            recv_sem=hop_r.at[n],
            device_id=(p - inner, hd),
            device_id_type=MESH,
        )

    def end_copy(n, sender, to, where):
        first, end = chunks[n]
        return pltpu.make_async_remote_copy(
            src_ref=ends.at[to, first:end],
            dst_ref=incoming.at[first:end, where, :],
            send_sem=end_s.at[n, to],
            recv_sem=end_r.at[n, sender],
            device_id=(o * inner + to, hd),
            device_id_type=MESH,
        )

    def pass_on(n):
        for h in range(*chunks[n]):
            leave[h] = (
                alone[inner - 1, h] + decays[inner - 1, h, 0:1] * carry[h].astype(F32)
            ).astype(BF16)
        hop_copy(n).start()

    def hand_back(n):
        first, end = chunks[n]
        for h in range(first, end):
            from_later = carry[h].astype(F32)
            ends[inner - 1, h] = carry[h]
            for j in range(inner - 1):
                ends[j, h] = (alone[j, h] + decays[j, h, 0:1] * from_later).astype(BF16)
        for j in range(inner):

            @pl.when(j != i)
            def _(j=j):
                end_copy(n, i, j, share).start()

        incoming[first:end, share, :] = ends[i, first:end]

    @pl.when(o == outer - 1)
    def _():
        carry[...] = jnp.zeros_like(carry)

    for n, (first, end) in enumerate(chunks):
        for j in range(inner):

            @pl.when(j != i)
            def _(j=j):
                if n == 0:
                    dec_copy(j, j).wait_recv()
                push_copy(n, j, j).wait_recv()

        for h in range(first, end):
            state = gath[inner - 1, h].astype(F32)
            decay = dgath[inner - 1, h : h + 1]
            for j in range(inner - 2, -1, -1):
                alone[j, h] = state
                decays[j, h] = jnp.broadcast_to(decay, (8, LANES))
                step = dgath[j, h : h + 1]
                state = gath[j, h].astype(F32) + step * state
                decay = decay * step
            alone[inner - 1, h] = state
            decays[inner - 1, h] = jnp.broadcast_to(decay, (8, LANES))

        @pl.when(o == outer - 1)
        def _(n=n):
            if outer > 1:
                pass_on(n)
            hand_back(n)

    for h in range(heads):
        at = cols[h]
        total = c[:, at]
        middle = total[tokens // 2 - 1 : tokens // 2]
        k_high, k_low = halves(k[:, at].astype(F32) * jnp.exp(middle - total))
        q_high, q_low = halves(q[:, at].astype(F32) * jnp.exp(total - middle))
        weight = product(
            jnp.concatenate([k_high, k_high], axis=1), jnp.concatenate([q_high, q_low], axis=1), 1, 1
        ) + product(k_low, q_high, 1, 1)
        weight = jnp.where(upper, weight, 0.0)
        gv_part[:, at] = product(both(weight, 1), twice(g[:, at], 0), 1, 0)
    gg_part[...] = product(twice(upper_b, 1), both(terms[...], 0), 1, 0)

    if outer > 1:

        @pl.when(o < outer - 1)
        def _():
            for n in range(len(chunks)):
                hop_copy(n).wait_recv()

                @pl.when(o > 0)
                def _(n=n):
                    pass_on(n)

                hand_back(n)

    for h in range(heads):
        turned[h] = s[h].T
        at = cols[h]
        tail_high, tail_low = halves(ktail[:, at])
        tails[h, :, 0:LANES] = tail_high
        tails[h, :, LANES:] = tail_low

    for n, (first, end) in enumerate(chunks):
        for j in range(inner):

            @pl.when(j != i)
            def _(j=j):
                end_copy(n, j, j, slice(j * part, (j + 1) * part)).wait_recv()

        for h in range(first, end):
            at = cols[h]
            gv[0:tokens, at] = (
                gv_part[:, at] + product(tails[h], twice(incoming[h], 1), 1, 1)
            ).astype(BF16)

    def edge_copy():
        return pltpu.make_async_remote_copy(
            src_ref=gv.at[0:EDGE],
            dst_ref=gv.at[tokens : tokens + EDGE],
            send_sem=edge_s,
            recv_sem=edge_r,
            device_id=(p - 1, hd),
            device_id_type=MESH,
        )

    @pl.when(p > 0)
    def _():
        edge_copy().start()
        before_copy().wait_recv()

    @pl.when(p == seqs - 1)
    def _():
        gv[tokens : tokens + EDGE] = jnp.zeros((EDGE, columns), BF16)

    rows = gv[0:tokens].astype(F32)
    x_f = x[...].astype(F32)
    for tap in range(taps):
        sums[tap : tap + 1] = jnp.sum(
            rows * x_f[EDGE - tap : EDGE - tap + tokens], axis=0, keepdims=True
        )

    def sum_copy(sender, to):
        return pltpu.make_async_remote_copy(
            src_ref=sums,
            dst_ref=all_sums.at[sender],
            send_sem=sum_s.at[to],
            recv_sem=sum_r.at[sender],
            device_id=(to, hd),
            device_id_type=MESH,
        )

    def send_sum(n, carried):
        sum_copy(p, lax.rem(p + n, seqs)).start()
        return carried

    lax.fori_loop(1, seqs, send_sum, 0)
    all_sums[p] = sums[...]

    loads[7].wait()

    def convolve(first, end):
        rows = gv[first : end + EDGE].astype(F32)
        result = w[0:1] * rows[: end - first]
        for tap in range(1, taps):
            result = result + w[tap : tap + 1] * rows[tap : tap + end - first]
        gi[first:end] = result.astype(BF16)

    def row_copy(sender, to):
        return pltpu.make_async_remote_copy(
            src_ref=gi.at[to * own_rows : (to + 1) * own_rows],
            dst_ref=gi_out.at[:, pl.ds(pl.multiple_of(sender * columns, LANES), columns)],
            send_sem=row_s.at[to],
            recv_sem=row_r.at[sender],
            device_id=(p, to),
            device_id_type=MESH,
        )

    def keep_copy(to):
        return pltpu.make_async_copy(
            gi.at[to * own_rows : (to + 1) * own_rows], gi_out.at[:, mine], row_s.at[to]
        )

    def hand_out(to):
        @pl.when(to != hd)
        def _():
            row_copy(hd, to).start()

        @pl.when(to == hd)
        def _():
            keep_copy(to).start()

    for to in range(groups - 1):
        convolve(to * own_rows, (to + 1) * own_rows)
        hand_out(to)

    for h in range(heads):
        at = cols[h]
        later = product(v[:, at], incoming[h], 1, 0)
        gk_out[:, at] = (gk_part[:, at] + scale[:, at] * later).astype(BF16)
        own = jnp.sum(incoming[h].astype(F32) * turned[h], axis=0, keepdims=True)
        gg = (
            gg_part[:, at]
            + product(strict_b, (ktail[:, at] * later).astype(BF16), 1, 0)
            + own * dec[h : h + 1]
        )
        gg_out[:, at] = gg.astype(BF16)

    @pl.when(p < seqs - 1)
    def _():
        edge_copy().wait_recv()

    convolve((groups - 1) * own_rows, tokens)
    hand_out(groups - 1)


    def take_sum(n, carried):
        other = lax.rem(p + n, seqs)
        sum_copy(other, other).wait_recv()
        return carried

    lax.fori_loop(1, seqs, take_sum, 0)
    added = lax.fori_loop(
        0, seqs, lambda n, value: value + all_sums[n], jnp.zeros((taps, columns), F32)
    )
    gw_out[...] = added

    for sender in range(groups):

        @pl.when(sender != hd)
        def _(sender=sender):
            row_copy(sender, sender).wait_recv()

    for to in range(groups):

        @pl.when(to != hd)
        def _(to=to):
            row_copy(hd, to).wait_send()

        @pl.when(to == hd)
        def _(to=to):
            keep_copy(to).wait()

    def sent_sum(n, carried):
        sum_copy(p, lax.rem(p + n, seqs)).wait_send()
        return carried

    lax.fori_loop(1, seqs, sent_sum, 0)
    for j in range(inner):

        @pl.when(j != i)
        def _(j=j):
            dec_copy(i, j).wait_send()
            for n in range(len(chunks)):
                push_copy(n, i, j).wait_send()
                end_copy(n, i, j, share).wait_send()

    if outer > 1:

        @pl.when(o > 0)
        def _():
            for n in range(len(chunks)):
                hop_copy(n).wait_send()

    @pl.when(p > 0)
    def _():
        edge_copy().wait_send()

    @pl.when(p < seqs - 1)
    def _():
        before_copy().wait_send()


def deliver(*refs):
    count = len(refs) // 2
    copies = [
        pltpu.make_async_copy(refs[n], refs[count + n], refs[-1].at[n]) for n in range(count)
    ]
    for copy in copies:
        copy.start()
    for copy in copies:
        copy.wait()


def solution(mesh):
    seqs, groups = mesh.shape["seq"], mesh.shape["head"]
    inner = 4 if seqs % 4 == 0 else 1

    def per_device(queries, key_rows, values, conv_input, log_gates, grad_output, saved_state, conv_kernel):
        tokens, columns = queries.shape
        heads = saved_state.shape[1]
        taps = conv_kernel.shape[0]
        part = LANES // inner
        flat = (tokens, columns)
        dma = pltpu.SemaphoreType.DMA
        vmem = pltpu.VMEM
        shapes = (
            jax.ShapeDtypeStruct(flat, BF16),
            jax.ShapeDtypeStruct(flat, BF16),
            jax.ShapeDtypeStruct(flat, BF16),
            jax.ShapeDtypeStruct((tokens // groups, columns * groups), BF16),
            jax.ShapeDtypeStruct((taps, columns), F32),
        )
        results = pl.pallas_call(
            functools.partial(body, seqs, groups, inner, heads, tokens, taps),
            out_shape=tuple(vmem(made.shape, made.dtype) for made in shapes),
            in_specs=[pl.BlockSpec(memory_space=pltpu.HBM)] * 8,
            out_specs=[pl.BlockSpec(memory_space=pltpu.VMEM)] * 5,
            scratch_shapes=[vmem(flat, BF16)] * 3
            + [vmem((tokens + EDGE, columns), BF16)]
            + [vmem(flat, BF16)] * 2
            + [
                vmem((heads, LANES, LANES), F32),
                vmem((taps, columns), F32),
                vmem((heads, LANES, LANES), F32),
                vmem((heads, tokens, 2 * LANES), BF16),
                vmem(flat, F32),
                vmem(flat, BF16),
                vmem(flat, BF16),
                vmem(flat, F32),
                vmem(flat, F32),
                vmem(flat, F32),
                vmem(flat, F32),
                vmem(flat, F32),
                vmem(flat, F32),
                vmem((heads, LANES, LANES), BF16),
                vmem((heads, LANES), F32),
                vmem((inner, heads, part, LANES), BF16),
                vmem((inner, heads, LANES), F32),
                vmem((inner, heads, part, LANES), F32),
                vmem((inner, heads, 8, LANES), F32),
                vmem((heads, part, LANES), BF16),
                vmem((heads, part, LANES), BF16),
                vmem((inner, heads, part, LANES), BF16),
                vmem((heads, LANES, LANES), BF16),
                vmem((tokens + EDGE, columns), BF16),
                vmem(flat, BF16),
                vmem((taps, columns), F32),
                vmem((seqs, taps, columns), F32),
                dma((8,)),
                dma((2, inner)),
                dma((2, inner)),
                dma((inner,)),
                dma((inner,)),
                dma((2,)),
                dma((2,)),
                dma((2, inner)),
                dma((2, inner)),
                dma,
                dma,
                dma,
                dma,
                dma((groups,)),
                dma((groups,)),
                dma((seqs,)),
                dma((seqs,)),
            ],
            compiler_params=pltpu.CompilerParams(
                collective_id=0, has_side_effects=True, vmem_limit_bytes=60 * 1024 * 1024
            ),
        )(queries, key_rows, values, conv_input, log_gates, grad_output, saved_state, conv_kernel)
        return pl.pallas_call(
            deliver,
            out_shape=shapes,
            in_specs=[pl.BlockSpec(memory_space=pltpu.VMEM)] * len(shapes),
            out_specs=[pl.BlockSpec(memory_space=pltpu.HBM)] * len(shapes),
            scratch_shapes=[dma((len(shapes),))],
        )(*results)

    return jax.shard_map(
        per_device,
        mesh=mesh,
        in_specs=(
            P("seq", "head"),
            P("seq", "head"),
            P("seq", "head"),
            P("seq", "head"),
            P("seq", "head"),
            P("seq", "head"),
            P("seq", "head", None, None),
            P(),
        ),
        out_specs=(
            P("seq", "head"),
            P("seq", "head"),
            P("seq", "head"),
            P(("seq", "head"), None),
            P(None, "head"),
        ),
        check_vma=False,
    )
```

```python
import functools

import jax
import jax.numpy as jnp
from jax import lax
from jax.experimental import pallas as pl
from jax.experimental.pallas import tpu as pltpu
from jax.sharding import PartitionSpec as P

MESH = pl.DeviceIdType.MESH
F32 = jnp.float32
BF16 = jnp.bfloat16
LANES = 128
EDGE = 16


def product(a, b, dim_a, dim_b):
    return lax.dot_general(
        a, b, (((dim_a,), (dim_b,)), ((), ())), preferred_element_type=F32
    )


def halves(x):
    high = x.astype(BF16)
    return high, (x - high.astype(F32)).astype(BF16)


def both(x, axis):
    return jnp.concatenate(halves(x), axis=axis)


def twice(x, axis):
    return jnp.concatenate([x, x], axis=axis)


def body(
    seqs, groups, inner, heads, tokens, taps,
    q_in, k_in, v_in, x_in, l_in, g_in, s_in, w_in,
    gq_out, gk_out, gg_out, gi_out, gw_out,
    q, k, v, x, l, g, s, w,
    turned, tails, c, qup, kdn, scale, ktail, terms, gk_part, gv_part, gg_part,
    push, dec, gath, dgath, alone, decays, carry, leave, ends, incoming,
    gv, gi, sums, all_sums,
    in_sem, push_s, push_r, dec_s, dec_r, hop_s, hop_r, end_s, end_r,
    before_s, before_r, edge_s, edge_r, row_s, row_r, sum_s, sum_r,
):
    p = lax.axis_index("seq")
    hd = lax.axis_index("head")
    o, i = p // inner, p % inner
    outer = seqs // inner
    part = LANES // inner
    columns = heads * LANES
    own_rows = tokens // groups
    half = heads // 2
    chunks = [(0, half), (half, heads)] if half else [(0, heads)]
    cols = [slice(h * LANES, (h + 1) * LANES) for h in range(heads)]

    mine = pl.ds(pl.multiple_of(hd * columns, LANES), columns)
    loads = [
        pltpu.make_async_copy(src, dst, in_sem.at[n])
        for n, (src, dst) in enumerate(
            [(l_in, l), (q_in, q), (g_in, g), (k_in, k), (v_in, v), (s_in.at[0], s), (x_in, x.at[EDGE:]), (w_in.at[:, mine], w)]
        )
    ]
    for load in loads:
        load.start()

    def greet(n, carried):
        pl.semaphore_signal(
            barrier, inc=1, device_id=(lax.rem(p + n, seqs), hd), device_id_type=MESH
        )
        return carried

    barrier = pltpu.get_barrier_semaphore()
    lax.fori_loop(1, seqs, greet, 0)
    for n in range(1, groups):
        pl.semaphore_signal(
            barrier, inc=1, device_id=(p, lax.rem(hd + n, groups)), device_id_type=MESH
        )

    row = lax.broadcasted_iota(jnp.int32, (tokens, tokens), 0)
    col = lax.broadcasted_iota(jnp.int32, (tokens, tokens), 1)
    lower = row >= col
    upper = col >= row
    lower_b = jnp.where(lower, 1.0, 0.0).astype(BF16)
    upper_b = jnp.where(upper, 1.0, 0.0).astype(BF16)
    strict_b = jnp.where(row > col, 1.0, 0.0).astype(BF16)

    loads[0].wait()
    total = product(lower_b, l[...], 1, 0)
    c[...] = total
    middle = total[tokens // 2 - 1 : tokens // 2]
    last = total[tokens - 1 : tokens]
    to_middle = jnp.exp(middle)
    grow = jnp.exp(total - middle)
    whole = jnp.exp(last)
    for h in range(heads):
        dec[h : h + 1] = whole[:, cols[h]]
    loads[1].wait()
    up = q[...].astype(F32) * grow
    qup[...] = up.astype(BF16)
    full = up * to_middle
    loads[2].wait()

    def push_copy(n, sender, to):
        first, end = chunks[n]
        return pltpu.make_async_remote_copy(
            src_ref=push.at[first:end, to * part : (to + 1) * part, :],
            dst_ref=gath.at[sender, first:end],
            send_sem=push_s.at[n, to],
            recv_sem=push_r.at[n, sender],
            device_id=(o * inner + to, hd),
            device_id_type=MESH,
        )

    def dec_copy(sender, to):
        return pltpu.make_async_remote_copy(
            src_ref=dec,
            dst_ref=dgath.at[sender],
            send_sem=dec_s.at[to],
            recv_sem=dec_r.at[sender],
            device_id=(o * inner + to, hd),
            device_id_type=MESH,
        )

    def before_copy():
        return pltpu.make_async_remote_copy(
            src_ref=x.at[tokens : tokens + EDGE],
            dst_ref=x.at[0:EDGE],
            send_sem=before_s,
            recv_sem=before_r,
            device_id=(p + 1, hd),
            device_id_type=MESH,
        )

    for n, (first, end) in enumerate(chunks):
        for h in range(first, end):
            push[h] = product(
                twice(g[:, cols[h]], 0), both(full[:, cols[h]], 0), 0, 0
            ).astype(BF16)
        if n == 0:
            pl.semaphore_wait(barrier, seqs - 1 + groups - 1)
        for j in range(inner):

            @pl.when(j != i)
            def _(j=j):
                if n == 0:
                    dec_copy(i, j).start()
                push_copy(n, i, j).start()

    loads[6].wait()

    @pl.when(p < seqs - 1)
    def _():
        before_copy().start()

    @pl.when(p == 0)
    def _():
        x[0:EDGE] = jnp.zeros((EDGE, columns), BF16)

    gath[i] = push[:, pl.ds(pl.multiple_of(i * part, part), part), :]
    dgath[i] = dec[...]

    loads[3].wait()
    loads[4].wait()
    loads[5].wait()
    total = c[...]
    middle = total[tokens // 2 - 1 : tokens // 2]
    last = total[tokens - 1 : tokens]
    down = k[...].astype(F32) * jnp.exp(middle - total)
    kdn[...] = down.astype(BF16)
    scale[...] = jnp.exp(last - total)
    ktail[...] = down * jnp.exp(last - middle)
    scores = []
    for h in range(heads):
        at = cols[h]
        g_h = g[:, at]
        score = jnp.where(lower, product(g_h, v[:, at], 1, 1), 0.0).astype(BF16)
        scores.append(score)
        total = c[:, at]
        middle = total[tokens // 2 - 1 : tokens // 2]
        from_start = product(twice(g_h, 1), both(s[h], 1), 1, 1) * jnp.exp(total)
        kdn_h = kdn[:, at]
        qup_h = qup[:, at]
        inside = product(score, kdn_h, 1, 0)
        back = product(score, qup_h, 0, 0)
        gq_out[:, at] = (jnp.exp(total - middle) * inside + from_start).astype(BF16)
        gk_part[:, at] = jnp.exp(middle - total) * back
        terms[:, at] = (
            qup_h.astype(F32) * inside - kdn_h.astype(F32) * back + q[:, at].astype(F32) * from_start
        )

    share = pl.ds(pl.multiple_of(i * part, part), part)

    def hop_copy(n):
        first, end = chunks[n]
        return pltpu.make_async_remote_copy(
            src_ref=leave.at[first:end],
            dst_ref=carry.at[first:end],
            send_sem=hop_s.at[n],
            recv_sem=hop_r.at[n],
            device_id=(p - inner, hd),
            device_id_type=MESH,
        )

    def end_copy(n, sender, to, where):
        first, end = chunks[n]
        return pltpu.make_async_remote_copy(
            src_ref=ends.at[to, first:end],
            dst_ref=incoming.at[first:end, where, :],
            send_sem=end_s.at[n, to],
            recv_sem=end_r.at[n, sender],
            device_id=(o * inner + to, hd),
            device_id_type=MESH,
        )

    def pass_on(n):
        for h in range(*chunks[n]):
            leave[h] = (
                alone[inner - 1, h] + decays[inner - 1, h, 0:1] * carry[h].astype(F32)
            ).astype(BF16)
        hop_copy(n).start()

    def hand_back(n):
        first, end = chunks[n]
        for h in range(first, end):
            from_later = carry[h].astype(F32)
            ends[inner - 1, h] = carry[h]
            for j in range(inner - 1):
                ends[j, h] = (alone[j, h] + decays[j, h, 0:1] * from_later).astype(BF16)
        for j in range(inner):

            @pl.when(j != i)
            def _(j=j):
                end_copy(n, i, j, share).start()

        incoming[first:end, share, :] = ends[i, first:end]

    @pl.when(o == outer - 1)
    def _():
        carry[...] = jnp.zeros_like(carry)

    for n, (first, end) in enumerate(chunks):
        for j in range(inner):

            @pl.when(j != i)
            def _(j=j):
                if n == 0:
                    dec_copy(j, j).wait_recv()
                push_copy(n, j, j).wait_recv()

        for h in range(first, end):
            state = gath[inner - 1, h].astype(F32)
            decay = dgath[inner - 1, h : h + 1]
            for j in range(inner - 2, -1, -1):
                alone[j, h] = state
                decays[j, h] = jnp.broadcast_to(decay, (8, LANES))
                step = dgath[j, h : h + 1]
                state = gath[j, h].astype(F32) + step * state
                decay = decay * step
            alone[inner - 1, h] = state
            decays[inner - 1, h] = jnp.broadcast_to(decay, (8, LANES))

        @pl.when(o == outer - 1)
        def _(n=n):
            if outer > 1:
                pass_on(n)
            hand_back(n)

    for h in range(heads):
        at = cols[h]
        total = c[:, at]
        middle = total[tokens // 2 - 1 : tokens // 2]
        k_high, k_low = halves(k[:, at].astype(F32) * jnp.exp(middle - total))
        q_high, q_low = halves(q[:, at].astype(F32) * jnp.exp(total - middle))
        weight = product(
            jnp.concatenate([k_high, k_high], axis=1), jnp.concatenate([q_high, q_low], axis=1), 1, 1
        ) + product(k_low, q_high, 1, 1)
        weight = jnp.where(upper, weight, 0.0)
        gv_part[:, at] = product(both(weight, 1), twice(g[:, at], 0), 1, 0)
    gg_part[...] = product(twice(upper_b, 1), both(terms[...], 0), 1, 0)

    if outer > 1:

        @pl.when(o < outer - 1)
        def _():
            for n in range(len(chunks)):
                hop_copy(n).wait_recv()

                @pl.when(o > 0)
                def _(n=n):
                    pass_on(n)

                hand_back(n)

    for h in range(heads):
        turned[h] = s[h].T
        at = cols[h]
        tail_high, tail_low = halves(ktail[:, at])
        tails[h, :, 0:LANES] = tail_high
        tails[h, :, LANES:] = tail_low

    for n, (first, end) in enumerate(chunks):
        for j in range(inner):

            @pl.when(j != i)
            def _(j=j):
                end_copy(n, j, j, slice(j * part, (j + 1) * part)).wait_recv()

        for h in range(first, end):
            at = cols[h]
            gv[0:tokens, at] = (
                gv_part[:, at] + product(tails[h], twice(incoming[h], 1), 1, 1)
            ).astype(BF16)

    def edge_copy():
        return pltpu.make_async_remote_copy(
            src_ref=gv.at[0:EDGE],
            dst_ref=gv.at[tokens : tokens + EDGE],
            send_sem=edge_s,
            recv_sem=edge_r,
            device_id=(p - 1, hd),
            device_id_type=MESH,
        )

    @pl.when(p > 0)
    def _():
        edge_copy().start()
        before_copy().wait_recv()

    @pl.when(p == seqs - 1)
    def _():
        gv[tokens : tokens + EDGE] = jnp.zeros((EDGE, columns), BF16)

    rows = gv[0:tokens].astype(F32)
    x_f = x[...].astype(F32)
    for tap in range(taps):
        sums[tap : tap + 1] = jnp.sum(
            rows * x_f[EDGE - tap : EDGE - tap + tokens], axis=0, keepdims=True
        )

    def sum_copy(sender, to):
        return pltpu.make_async_remote_copy(
            src_ref=sums,
            dst_ref=all_sums.at[sender],
            send_sem=sum_s.at[to],
            recv_sem=sum_r.at[sender],
            device_id=(to, hd),
            device_id_type=MESH,
        )

    def send_sum(n, carried):
        sum_copy(p, lax.rem(p + n, seqs)).start()
        return carried

    lax.fori_loop(1, seqs, send_sum, 0)
    all_sums[p] = sums[...]

    loads[7].wait()

    def convolve(first, end):
        rows = gv[first : end + EDGE].astype(F32)
        result = w[0:1] * rows[: end - first]
        for tap in range(1, taps):
            result = result + w[tap : tap + 1] * rows[tap : tap + end - first]
        gi[first:end] = result.astype(BF16)

    def row_copy(sender, to):
        return pltpu.make_async_remote_copy(
            src_ref=gi.at[to * own_rows : (to + 1) * own_rows],
            dst_ref=gi_out.at[:, pl.ds(pl.multiple_of(sender * columns, LANES), columns)],
            send_sem=row_s.at[to],
            recv_sem=row_r.at[sender],
            device_id=(p, to),
            device_id_type=MESH,
        )

    def keep_copy(to):
        return pltpu.make_async_copy(
            gi.at[to * own_rows : (to + 1) * own_rows], gi_out.at[:, mine], row_s.at[to]
        )

    def hand_out(to):
        @pl.when(to != hd)
        def _():
            row_copy(hd, to).start()

        @pl.when(to == hd)
        def _():
            keep_copy(to).start()

    for to in range(groups - 1):
        convolve(to * own_rows, (to + 1) * own_rows)
        hand_out(to)

    for h in range(heads):
        at = cols[h]
        later = product(v[:, at], incoming[h], 1, 0)
        gk_out[:, at] = (gk_part[:, at] + scale[:, at] * later).astype(BF16)
        own = jnp.sum(incoming[h].astype(F32) * turned[h], axis=0, keepdims=True)
        gg = (
            gg_part[:, at]
            + product(strict_b, (ktail[:, at] * later).astype(BF16), 1, 0)
            + own * dec[h : h + 1]
        )
        gg_out[:, at] = gg.astype(BF16)

    @pl.when(p < seqs - 1)
    def _():
        edge_copy().wait_recv()

    convolve((groups - 1) * own_rows, tokens)
    hand_out(groups - 1)


    def take_sum(n, carried):
        other = lax.rem(p + n, seqs)
        sum_copy(other, other).wait_recv()
        return carried

    lax.fori_loop(1, seqs, take_sum, 0)
    added = lax.fori_loop(
        0, seqs, lambda n, value: value + all_sums[n], jnp.zeros((taps, columns), F32)
    )
    gw_out[...] = added

    for sender in range(groups):

        @pl.when(sender != hd)
        def _(sender=sender):
            row_copy(sender, sender).wait_recv()

    for to in range(groups):

        @pl.when(to != hd)
        def _(to=to):
            row_copy(hd, to).wait_send()

        @pl.when(to == hd)
        def _(to=to):
            keep_copy(to).wait()

    def sent_sum(n, carried):
        sum_copy(p, lax.rem(p + n, seqs)).wait_send()
        return carried

    lax.fori_loop(1, seqs, sent_sum, 0)
    for j in range(inner):

        @pl.when(j != i)
        def _(j=j):
            dec_copy(i, j).wait_send()
            for n in range(len(chunks)):
                push_copy(n, i, j).wait_send()
                end_copy(n, i, j, share).wait_send()

    if outer > 1:

        @pl.when(o > 0)
        def _():
            for n in range(len(chunks)):
                hop_copy(n).wait_send()

    @pl.when(p > 0)
    def _():
        edge_copy().wait_send()

    @pl.when(p < seqs - 1)
    def _():
        before_copy().wait_send()


def deliver(*refs):
    count = len(refs) // 2
    copies = [
        pltpu.make_async_copy(refs[n], refs[count + n], refs[-1].at[n]) for n in range(count)
    ]
    for copy in copies:
        copy.start()
    for copy in copies:
        copy.wait()


def solution(mesh):
    seqs, groups = mesh.shape["seq"], mesh.shape["head"]
    inner = 4 if seqs % 4 == 0 else 1

    def per_device(queries, key_rows, values, conv_input, log_gates, grad_output, saved_state, conv_kernel):
        tokens, columns = queries.shape
        heads = saved_state.shape[1]
        taps = conv_kernel.shape[0]
        part = LANES // inner
        flat = (tokens, columns)
        dma = pltpu.SemaphoreType.DMA
        vmem = pltpu.VMEM
        shapes = (
            jax.ShapeDtypeStruct(flat, BF16),
            jax.ShapeDtypeStruct(flat, BF16),
            jax.ShapeDtypeStruct(flat, BF16),
            jax.ShapeDtypeStruct((tokens // groups, columns * groups), BF16),
            jax.ShapeDtypeStruct((taps, columns), F32),
        )
        results = pl.pallas_call(
            functools.partial(body, seqs, groups, inner, heads, tokens, taps),
            out_shape=tuple(vmem(made.shape, made.dtype) for made in shapes),
            in_specs=[pl.BlockSpec(memory_space=pltpu.HBM)] * 8,
            out_specs=[pl.BlockSpec(memory_space=pltpu.VMEM)] * 5,
            scratch_shapes=[vmem(flat, BF16)] * 3
            + [vmem((tokens + EDGE, columns), BF16)]
            + [vmem(flat, BF16)] * 2
            + [
                vmem((heads, LANES, LANES), F32),
                vmem((taps, columns), F32),
                vmem((heads, LANES, LANES), F32),
                vmem((heads, tokens, 2 * LANES), BF16),
                vmem(flat, F32),
                vmem(flat, BF16),
                vmem(flat, BF16),
                vmem(flat, F32),
                vmem(flat, F32),
                vmem(flat, F32),
                vmem(flat, F32),
                vmem(flat, F32),
                vmem(flat, F32),
                vmem((heads, LANES, LANES), BF16),
                vmem((heads, LANES), F32),
                vmem((inner, heads, part, LANES), BF16),
                vmem((inner, heads, LANES), F32),
                vmem((inner, heads, part, LANES), F32),
                vmem((inner, heads, 8, LANES), F32),
                vmem((heads, part, LANES), BF16),
                vmem((heads, part, LANES), BF16),
                vmem((inner, heads, part, LANES), BF16),
                vmem((heads, LANES, LANES), BF16),
                vmem((tokens + EDGE, columns), BF16),
                vmem(flat, BF16),
                vmem((taps, columns), F32),
                vmem((seqs, taps, columns), F32),
                dma((8,)),
                dma((2, inner)),
                dma((2, inner)),
                dma((inner,)),
                dma((inner,)),
                dma((2,)),
                dma((2,)),
                dma((2, inner)),
                dma((2, inner)),
                dma,
                dma,
                dma,
                dma,
                dma((groups,)),
                dma((groups,)),
                dma((seqs,)),
                dma((seqs,)),
            ],
            compiler_params=pltpu.CompilerParams(
                collective_id=0, has_side_effects=True, vmem_limit_bytes=60 * 1024 * 1024
            ),
        )(queries, key_rows, values, conv_input, log_gates, grad_output, saved_state, conv_kernel)
        return pl.pallas_call(
            deliver,
            out_shape=shapes,
            in_specs=[pl.BlockSpec(memory_space=pltpu.VMEM)] * len(shapes),
            out_specs=[pl.BlockSpec(memory_space=pltpu.HBM)] * len(shapes),
            scratch_shapes=[dma((len(shapes),))],
            compiler_params=pltpu.CompilerParams(vmem_limit_bytes=2 * 1024 * 1024),
        )(*results)

    return jax.shard_map(
        per_device,
        mesh=mesh,
        in_specs=(
            P("seq", "head"),
            P("seq", "head"),
            P("seq", "head"),
            P("seq", "head"),
            P("seq", "head"),
            P("seq", "head"),
            P("seq", "head", None, None),
            P(),
        ),
        out_specs=(
            P("seq", "head"),
            P("seq", "head"),
            P("seq", "head"),
            P(("seq", "head"), None),
            P(None, "head"),
        ),
        check_vma=False,
    )
```

```python
import functools

import jax
import jax.numpy as jnp
from jax import lax
from jax.experimental import pallas as pl
from jax.experimental.pallas import tpu as pltpu
from jax.sharding import PartitionSpec as P

MESH = pl.DeviceIdType.MESH
F32 = jnp.float32
BF16 = jnp.bfloat16
LANES = 128
EDGE = 16


def product(a, b, dim_a, dim_b):
    return lax.dot_general(
        a, b, (((dim_a,), (dim_b,)), ((), ())), preferred_element_type=F32
    )


def halves(x):
    high = x.astype(BF16)
    return high, (x - high.astype(F32)).astype(BF16)


def both(x, axis):
    return jnp.concatenate(halves(x), axis=axis)


def twice(x, axis):
    return jnp.concatenate([x, x], axis=axis)


def spans(heads):
    count = 3 if heads % 3 == 0 else 1
    width = heads // count
    return [(n * width, (n + 1) * width) for n in range(count)]


def body(
    seqs, groups, inner, heads, tokens, taps,
    q_in, k_in, v_in, x_in, l_in, g_in, s_in, w_in,
    gq_out, gk_out, gg_out, gi_out, gw_out,
    q, k, v, x, l, g, s, w,
    turned, tails, c, qup, kdn, scale, ktail, terms, gk_part, gv_part, gg_part,
    push, dec, gath, dgath, alone, decays, carry, leave, ends, incoming,
    gv, gi, sums, all_sums,
    in_sem, push_s, push_r, dec_s, dec_r, hop_s, hop_r, end_s, end_r,
    before_s, before_r, edge_s, edge_r, row_s, row_r, sum_s, sum_r,
):
    p = lax.axis_index("seq")
    hd = lax.axis_index("head")
    o, i = p // inner, p % inner
    outer = seqs // inner
    part = LANES // inner
    columns = heads * LANES
    own_rows = tokens // groups
    half = heads // 2
    chunks = spans(heads)
    cols = [slice(h * LANES, (h + 1) * LANES) for h in range(heads)]

    mine = pl.ds(pl.multiple_of(hd * columns, LANES), columns)
    loads = [
        pltpu.make_async_copy(src, dst, in_sem.at[n])
        for n, (src, dst) in enumerate(
            [(l_in, l), (q_in, q), (g_in, g), (k_in, k), (v_in, v), (s_in.at[0], s), (x_in, x.at[EDGE:]), (w_in.at[:, mine], w)]
        )
    ]
    for load in loads:
        load.start()

    def greet(n, carried):
        pl.semaphore_signal(
            barrier, inc=1, device_id=(lax.rem(p + n, seqs), hd), device_id_type=MESH
        )
        return carried

    barrier = pltpu.get_barrier_semaphore()
    lax.fori_loop(1, seqs, greet, 0)
    for n in range(1, groups):
        pl.semaphore_signal(
            barrier, inc=1, device_id=(p, lax.rem(hd + n, groups)), device_id_type=MESH
        )

    row = lax.broadcasted_iota(jnp.int32, (tokens, tokens), 0)
    col = lax.broadcasted_iota(jnp.int32, (tokens, tokens), 1)
    lower = row >= col
    upper = col >= row
    lower_b = jnp.where(lower, 1.0, 0.0).astype(BF16)
    upper_b = jnp.where(upper, 1.0, 0.0).astype(BF16)
    strict_b = jnp.where(row > col, 1.0, 0.0).astype(BF16)

    loads[0].wait()
    total = product(lower_b, l[...], 1, 0)
    c[...] = total
    middle = total[tokens // 2 - 1 : tokens // 2]
    last = total[tokens - 1 : tokens]
    to_middle = jnp.exp(middle)
    grow = jnp.exp(total - middle)
    whole = jnp.exp(last)
    for h in range(heads):
        dec[h : h + 1] = whole[:, cols[h]]
    loads[1].wait()
    up = q[...].astype(F32) * grow
    qup[...] = up.astype(BF16)
    full = up * to_middle
    loads[2].wait()

    def push_copy(n, sender, to):
        first, end = chunks[n]
        return pltpu.make_async_remote_copy(
            src_ref=push.at[first:end, to * part : (to + 1) * part, :],
            dst_ref=gath.at[sender, first:end],
            send_sem=push_s.at[n, to],
            recv_sem=push_r.at[n, sender],
            device_id=(o * inner + to, hd),
            device_id_type=MESH,
        )

    def dec_copy(sender, to):
        return pltpu.make_async_remote_copy(
            src_ref=dec,
            dst_ref=dgath.at[sender],
            send_sem=dec_s.at[to],
            recv_sem=dec_r.at[sender],
            device_id=(o * inner + to, hd),
            device_id_type=MESH,
        )

    def before_copy():
        return pltpu.make_async_remote_copy(
            src_ref=x.at[tokens : tokens + EDGE],
            dst_ref=x.at[0:EDGE],
            send_sem=before_s,
            recv_sem=before_r,
            device_id=(p + 1, hd),
            device_id_type=MESH,
        )

    for n, (first, end) in enumerate(chunks):
        for h in range(first, end):
            push[h] = product(
                twice(g[:, cols[h]], 0), both(full[:, cols[h]], 0), 0, 0
            ).astype(BF16)
        if n == 0:
            pl.semaphore_wait(barrier, seqs - 1 + groups - 1)
        for j in range(inner):

            @pl.when(j != i)
            def _(j=j):
                if n == 0:
                    dec_copy(i, j).start()
                push_copy(n, i, j).start()

    gath[i] = push[:, pl.ds(pl.multiple_of(i * part, part), part), :]
    dgath[i] = dec[...]

    loads[3].wait()
    loads[4].wait()
    loads[5].wait()
    total = c[...]
    middle = total[tokens // 2 - 1 : tokens // 2]
    last = total[tokens - 1 : tokens]
    down = k[...].astype(F32) * jnp.exp(middle - total)
    kdn[...] = down.astype(BF16)
    scale[...] = jnp.exp(last - total)
    ktail[...] = down * jnp.exp(last - middle)

    def inside_block(h):
        at = cols[h]
        g_h = g[:, at]
        score = jnp.where(lower, product(g_h, v[:, at], 1, 1), 0.0).astype(BF16)
        total = c[:, at]
        middle = total[tokens // 2 - 1 : tokens // 2]
        from_start = product(twice(g_h, 1), both(s[h], 1), 1, 1) * jnp.exp(total)
        kdn_h = kdn[:, at]
        qup_h = qup[:, at]
        inside = product(score, kdn_h, 1, 0)
        back = product(score, qup_h, 0, 0)
        gq_out[:, at] = (jnp.exp(total - middle) * inside + from_start).astype(BF16)
        gk_part[:, at] = jnp.exp(middle - total) * back
        terms[:, at] = (
            qup_h.astype(F32) * inside - kdn_h.astype(F32) * back + q[:, at].astype(F32) * from_start
        )


    for h in range(half):
        inside_block(h)

    share = pl.ds(pl.multiple_of(i * part, part), part)

    def hop_copy(n):
        first, end = chunks[n]
        return pltpu.make_async_remote_copy(
            src_ref=leave.at[first:end],
            dst_ref=carry.at[first:end],
            send_sem=hop_s.at[n],
            recv_sem=hop_r.at[n],
            device_id=(p - inner, hd),
            device_id_type=MESH,
        )

    def end_copy(n, sender, to, where):
        first, end = chunks[n]
        return pltpu.make_async_remote_copy(
            src_ref=ends.at[to, first:end],
            dst_ref=incoming.at[first:end, where, :],
            send_sem=end_s.at[n, to],
            recv_sem=end_r.at[n, sender],
            device_id=(o * inner + to, hd),
            device_id_type=MESH,
        )

    def pass_on(n):
        for h in range(*chunks[n]):
            leave[h] = (
                alone[inner - 1, h] + decays[inner - 1, h, 0:1] * carry[h].astype(F32)
            ).astype(BF16)
        hop_copy(n).start()

    def hand_back(n):
        first, end = chunks[n]
        for h in range(first, end):
            from_later = carry[h].astype(F32)
            ends[inner - 1, h] = carry[h]
            for j in range(inner - 1):
                ends[j, h] = (alone[j, h] + decays[j, h, 0:1] * from_later).astype(BF16)
        for j in range(inner):

            @pl.when(j != i)
            def _(j=j):
                end_copy(n, i, j, share).start()

        incoming[first:end, share, :] = ends[i, first:end]

    @pl.when(o == outer - 1)
    def _():
        carry[...] = jnp.zeros_like(carry)

    for n, (first, end) in enumerate(chunks):
        for j in range(inner):

            @pl.when(j != i)
            def _(j=j):
                if n == 0:
                    dec_copy(j, j).wait_recv()
                push_copy(n, j, j).wait_recv()

        for h in range(first, end):
            state = gath[inner - 1, h].astype(F32)
            decay = dgath[inner - 1, h : h + 1]
            for j in range(inner - 2, -1, -1):
                alone[j, h] = state
                decays[j, h] = jnp.broadcast_to(decay, (8, LANES))
                step = dgath[j, h : h + 1]
                state = gath[j, h].astype(F32) + step * state
                decay = decay * step
            alone[inner - 1, h] = state
            decays[inner - 1, h] = jnp.broadcast_to(decay, (8, LANES))

        @pl.when(o == outer - 1)
        def _(n=n):
            if outer > 1:
                pass_on(n)
            hand_back(n)

    def values_part(h):
        at = cols[h]
        total = c[:, at]
        middle = total[tokens // 2 - 1 : tokens // 2]
        k_high, k_low = halves(k[:, at].astype(F32) * jnp.exp(middle - total))
        q_high, q_low = halves(q[:, at].astype(F32) * jnp.exp(total - middle))
        weight = product(
            jnp.concatenate([k_high, k_high], axis=1), jnp.concatenate([q_high, q_low], axis=1), 1, 1
        ) + product(k_low, q_high, 1, 1)
        weight = jnp.where(upper, weight, 0.0)
        gv_part[:, at] = product(both(weight, 1), twice(g[:, at], 0), 1, 0)

    loads[6].wait()

    @pl.when(p < seqs - 1)
    def _():
        before_copy().start()

    @pl.when(p == 0)
    def _():
        x[0:EDGE] = jnp.zeros((EDGE, columns), BF16)

    for h in range(half, heads):
        inside_block(h)
    for h in range(half):
        values_part(h)

    if outer > 1:

        @pl.when(o < outer - 1)
        def _():
            for n in range(len(chunks)):
                hop_copy(n).wait_recv()

                @pl.when(o > 0)
                def _(n=n):
                    pass_on(n)

                hand_back(n)

    for h in range(half, heads):
        values_part(h)
    for h in range(heads):
        turned[h] = s[h].T
        at = cols[h]
        tail_high, tail_low = halves(ktail[:, at])
        tails[h, :, 0:LANES] = tail_high
        tails[h, :, LANES:] = tail_low

    for n, (first, end) in enumerate(chunks):
        for j in range(inner):

            @pl.when(j != i)
            def _(j=j):
                end_copy(n, j, j, slice(j * part, (j + 1) * part)).wait_recv()

        for h in range(first, end):
            at = cols[h]
            gv[0:tokens, at] = (
                gv_part[:, at] + product(tails[h], twice(incoming[h], 1), 1, 1)
            ).astype(BF16)

    def edge_copy():
        return pltpu.make_async_remote_copy(
            src_ref=gv.at[0:EDGE],
            dst_ref=gv.at[tokens : tokens + EDGE],
            send_sem=edge_s,
            recv_sem=edge_r,
            device_id=(p - 1, hd),
            device_id_type=MESH,
        )

    @pl.when(p > 0)
    def _():
        edge_copy().start()
        before_copy().wait_recv()

    @pl.when(p == seqs - 1)
    def _():
        gv[tokens : tokens + EDGE] = jnp.zeros((EDGE, columns), BF16)

    rows = gv[0:tokens].astype(F32)
    x_f = x[...].astype(F32)
    for tap in range(taps):
        sums[tap : tap + 1] = jnp.sum(
            rows * x_f[EDGE - tap : EDGE - tap + tokens], axis=0, keepdims=True
        )

    def sum_copy(sender, to):
        return pltpu.make_async_remote_copy(
            src_ref=sums,
            dst_ref=all_sums.at[sender],
            send_sem=sum_s.at[to],
            recv_sem=sum_r.at[sender],
            device_id=(to, hd),
            device_id_type=MESH,
        )

    def send_sum(n, carried):
        sum_copy(p, lax.rem(p + n, seqs)).start()
        return carried

    lax.fori_loop(1, seqs, send_sum, 0)
    all_sums[p] = sums[...]

    loads[7].wait()

    def convolve(first, end):
        rows = gv[first : end + EDGE].astype(F32)
        result = w[0:1] * rows[: end - first]
        for tap in range(1, taps):
            result = result + w[tap : tap + 1] * rows[tap : tap + end - first]
        gi[first:end] = result.astype(BF16)

    def row_copy(sender, to):
        return pltpu.make_async_remote_copy(
            src_ref=gi.at[to * own_rows : (to + 1) * own_rows],
            dst_ref=gi_out.at[:, pl.ds(pl.multiple_of(sender * columns, LANES), columns)],
            send_sem=row_s.at[to],
            recv_sem=row_r.at[sender],
            device_id=(p, to),
            device_id_type=MESH,
        )

    def keep_copy(to):
        return pltpu.make_async_copy(
            gi.at[to * own_rows : (to + 1) * own_rows], gi_out.at[:, mine], row_s.at[to]
        )

    def hand_out(to):
        @pl.when(to != hd)
        def _():
            row_copy(hd, to).start()

        @pl.when(to == hd)
        def _():
            keep_copy(to).start()

    for to in range(groups - 1):
        convolve(to * own_rows, (to + 1) * own_rows)
        hand_out(to)

    gg_part[...] = product(twice(upper_b, 1), both(terms[...], 0), 1, 0)
    for h in range(heads):
        at = cols[h]
        later = product(v[:, at], incoming[h], 1, 0)
        gk_out[:, at] = (gk_part[:, at] + scale[:, at] * later).astype(BF16)
        own = jnp.sum(incoming[h].astype(F32) * turned[h], axis=0, keepdims=True)
        gg = (
            gg_part[:, at]
            + product(strict_b, (ktail[:, at] * later).astype(BF16), 1, 0)
            + own * dec[h : h + 1]
        )
        gg_out[:, at] = gg.astype(BF16)

    @pl.when(p < seqs - 1)
    def _():
        edge_copy().wait_recv()

    convolve((groups - 1) * own_rows, tokens)
    hand_out(groups - 1)


    def take_sum(n, carried):
        other = lax.rem(p + n, seqs)
        sum_copy(other, other).wait_recv()
        return carried

    lax.fori_loop(1, seqs, take_sum, 0)
    added = lax.fori_loop(
        0, seqs, lambda n, value: value + all_sums[n], jnp.zeros((taps, columns), F32)
    )
    gw_out[...] = added

    for sender in range(groups):

        @pl.when(sender != hd)
        def _(sender=sender):
            row_copy(sender, sender).wait_recv()

    for to in range(groups):

        @pl.when(to != hd)
        def _(to=to):
            row_copy(hd, to).wait_send()

        @pl.when(to == hd)
        def _(to=to):
            keep_copy(to).wait()

    def sent_sum(n, carried):
        sum_copy(p, lax.rem(p + n, seqs)).wait_send()
        return carried

    lax.fori_loop(1, seqs, sent_sum, 0)
    for j in range(inner):

        @pl.when(j != i)
        def _(j=j):
            dec_copy(i, j).wait_send()
            for n in range(len(chunks)):
                push_copy(n, i, j).wait_send()
                end_copy(n, i, j, share).wait_send()

    if outer > 1:

        @pl.when(o > 0)
        def _():
            for n in range(len(chunks)):
                hop_copy(n).wait_send()

    @pl.when(p > 0)
    def _():
        edge_copy().wait_send()

    @pl.when(p < seqs - 1)
    def _():
        before_copy().wait_send()


def deliver(*refs):
    count = len(refs) // 2
    copies = [
        pltpu.make_async_copy(refs[n], refs[count + n], refs[-1].at[n]) for n in range(count)
    ]
    for copy in copies:
        copy.start()
    for copy in copies:
        copy.wait()


def solution(mesh):
    seqs, groups = mesh.shape["seq"], mesh.shape["head"]
    inner = 4 if seqs % 4 == 0 else 1

    def per_device(queries, key_rows, values, conv_input, log_gates, grad_output, saved_state, conv_kernel):
        tokens, columns = queries.shape
        heads = saved_state.shape[1]
        taps = conv_kernel.shape[0]
        part = LANES // inner
        flat = (tokens, columns)
        dma = pltpu.SemaphoreType.DMA
        vmem = pltpu.VMEM
        shapes = (
            jax.ShapeDtypeStruct(flat, BF16),
            jax.ShapeDtypeStruct(flat, BF16),
            jax.ShapeDtypeStruct(flat, BF16),
            jax.ShapeDtypeStruct((tokens // groups, columns * groups), BF16),
            jax.ShapeDtypeStruct((taps, columns), F32),
        )
        results = pl.pallas_call(
            functools.partial(body, seqs, groups, inner, heads, tokens, taps),
            out_shape=tuple(vmem(made.shape, made.dtype) for made in shapes),
            in_specs=[pl.BlockSpec(memory_space=pltpu.HBM)] * 8,
            out_specs=[pl.BlockSpec(memory_space=pltpu.VMEM)] * 5,
            scratch_shapes=[vmem(flat, BF16)] * 3
            + [vmem((tokens + EDGE, columns), BF16)]
            + [vmem(flat, BF16)] * 2
            + [
                vmem((heads, LANES, LANES), F32),
                vmem((taps, columns), F32),
                vmem((heads, LANES, LANES), F32),
                vmem((heads, tokens, 2 * LANES), BF16),
                vmem(flat, F32),
                vmem(flat, BF16),
                vmem(flat, BF16),
                vmem(flat, F32),
                vmem(flat, F32),
                vmem(flat, F32),
                vmem(flat, F32),
                vmem(flat, F32),
                vmem(flat, F32),
                vmem((heads, LANES, LANES), BF16),
                vmem((heads, LANES), F32),
                vmem((inner, heads, part, LANES), BF16),
                vmem((inner, heads, LANES), F32),
                vmem((inner, heads, part, LANES), F32),
                vmem((inner, heads, 8, LANES), F32),
                vmem((heads, part, LANES), BF16),
                vmem((heads, part, LANES), BF16),
                vmem((inner, heads, part, LANES), BF16),
                vmem((heads, LANES, LANES), BF16),
                vmem((tokens + EDGE, columns), BF16),
                vmem(flat, BF16),
                vmem((taps, columns), F32),
                vmem((seqs, taps, columns), F32),
                dma((8,)),
                dma((len(spans(heads)), inner)),
                dma((len(spans(heads)), inner)),
                dma((inner,)),
                dma((inner,)),
                dma((len(spans(heads)),)),
                dma((len(spans(heads)),)),
                dma((len(spans(heads)), inner)),
                dma((len(spans(heads)), inner)),
                dma,
                dma,
                dma,
                dma,
                dma((groups,)),
                dma((groups,)),
                dma((seqs,)),
                dma((seqs,)),
            ],
            compiler_params=pltpu.CompilerParams(
                collective_id=0, has_side_effects=True, vmem_limit_bytes=60 * 1024 * 1024
            ),
        )(queries, key_rows, values, conv_input, log_gates, grad_output, saved_state, conv_kernel)
        return pl.pallas_call(
            deliver,
            out_shape=shapes,
            in_specs=[pl.BlockSpec(memory_space=pltpu.VMEM)] * len(shapes),
            out_specs=[pl.BlockSpec(memory_space=pltpu.HBM)] * len(shapes),
            scratch_shapes=[dma((len(shapes),))],
            compiler_params=pltpu.CompilerParams(vmem_limit_bytes=2 * 1024 * 1024),
        )(*results)

    return jax.shard_map(
        per_device,
        mesh=mesh,
        in_specs=(
            P("seq", "head"),
            P("seq", "head"),
            P("seq", "head"),
            P("seq", "head"),
            P("seq", "head"),
            P("seq", "head"),
            P("seq", "head", None, None),
            P(),
        ),
        out_specs=(
            P("seq", "head"),
            P("seq", "head"),
            P("seq", "head"),
            P(("seq", "head"), None),
            P(None, "head"),
        ),
        check_vma=False,
    )
```

```python
import functools

import jax
import jax.numpy as jnp
from jax import lax
from jax.experimental import pallas as pl
from jax.experimental.pallas import tpu as pltpu
from jax.sharding import PartitionSpec as P

MESH = pl.DeviceIdType.MESH
F32 = jnp.float32
BF16 = jnp.bfloat16
LANES = 128
EDGE = 16


def product(a, b, dim_a, dim_b):
    return lax.dot_general(
        a, b, (((dim_a,), (dim_b,)), ((), ())), preferred_element_type=F32
    )


def halves(x):
    high = x.astype(BF16)
    return high, (x - high.astype(F32)).astype(BF16)


def both(x, axis):
    return jnp.concatenate(halves(x), axis=axis)


def twice(x, axis):
    return jnp.concatenate([x, x], axis=axis)


def spans(heads):
    count = 3 if heads % 3 == 0 else 1
    width = heads // count
    return [(n * width, (n + 1) * width) for n in range(count)]


def body(
    seqs, groups, inner, heads, tokens, taps,
    q_in, k_in, v_in, x_in, l_in, g_in, s_in, w_in,
    gq_out, gk_out, gg_out, gi_out, gw_out,
    q, k, v, x, l, g, s, w,
    turned, tails, c, qup, kdn, scale, ktail, terms, gk_part, gv_part, gg_part,
    push, dec, gath, dgath, alone, decays, carry, leave, ends, incoming,
    gv, gi, sums, all_sums, group_sum, group_sums,
    in_sem, push_s, push_r, dec_s, dec_r, hop_s, hop_r, end_s, end_r,
    before_s, before_r, edge_s, edge_r, row_s, row_r, sum_s, sum_r, total_s, total_r,
):
    p = lax.axis_index("seq")
    hd = lax.axis_index("head")
    o, i = p // inner, p % inner
    outer = seqs // inner
    part = LANES // inner
    columns = heads * LANES
    own_rows = tokens // groups
    half = heads // 2
    chunks = spans(heads)
    cols = [slice(h * LANES, (h + 1) * LANES) for h in range(heads)]

    mine = pl.ds(pl.multiple_of(hd * columns, LANES), columns)
    loads = [
        pltpu.make_async_copy(src, dst, in_sem.at[n])
        for n, (src, dst) in enumerate(
            [(l_in, l), (q_in, q), (g_in, g), (k_in, k), (v_in, v), (s_in.at[0], s), (x_in, x.at[EDGE:]), (w_in.at[:, mine], w)]
        )
    ]
    for load in loads:
        load.start()

    def greet(n, carried):
        pl.semaphore_signal(
            barrier, inc=1, device_id=(lax.rem(p + n, seqs), hd), device_id_type=MESH
        )
        return carried

    barrier = pltpu.get_barrier_semaphore()
    lax.fori_loop(1, seqs, greet, 0)
    for n in range(1, groups):
        pl.semaphore_signal(
            barrier, inc=1, device_id=(p, lax.rem(hd + n, groups)), device_id_type=MESH
        )

    row = lax.broadcasted_iota(jnp.int32, (tokens, tokens), 0)
    col = lax.broadcasted_iota(jnp.int32, (tokens, tokens), 1)
    lower = row >= col
    upper = col >= row
    lower_b = jnp.where(lower, 1.0, 0.0).astype(BF16)
    upper_b = jnp.where(upper, 1.0, 0.0).astype(BF16)
    strict_b = jnp.where(row > col, 1.0, 0.0).astype(BF16)

    loads[0].wait()
    total = product(lower_b, l[...], 1, 0)
    c[...] = total
    middle = total[tokens // 2 - 1 : tokens // 2]
    last = total[tokens - 1 : tokens]
    to_middle = jnp.exp(middle)
    grow = jnp.exp(total - middle)
    whole = jnp.exp(last)
    for h in range(heads):
        dec[h : h + 1] = whole[:, cols[h]]
    loads[1].wait()
    up = q[...].astype(F32) * grow
    qup[...] = up.astype(BF16)
    full = up * to_middle
    loads[2].wait()

    def push_copy(n, sender, to):
        first, end = chunks[n]
        return pltpu.make_async_remote_copy(
            src_ref=push.at[first:end, to * part : (to + 1) * part, :],
            dst_ref=gath.at[sender, first:end],
            send_sem=push_s.at[n, to],
            recv_sem=push_r.at[n, sender],
            device_id=(o * inner + to, hd),
            device_id_type=MESH,
        )

    def dec_copy(sender, to):
        return pltpu.make_async_remote_copy(
            src_ref=dec,
            dst_ref=dgath.at[sender],
            send_sem=dec_s.at[to],
            recv_sem=dec_r.at[sender],
            device_id=(o * inner + to, hd),
            device_id_type=MESH,
        )

    def before_copy():
        return pltpu.make_async_remote_copy(
            src_ref=x.at[tokens : tokens + EDGE],
            dst_ref=x.at[0:EDGE],
            send_sem=before_s,
            recv_sem=before_r,
            device_id=(p + 1, hd),
            device_id_type=MESH,
        )

    for n, (first, end) in enumerate(chunks):
        for h in range(first, end):
            push[h] = product(
                twice(g[:, cols[h]], 0), both(full[:, cols[h]], 0), 0, 0
            ).astype(BF16)
        if n == 0:
            pl.semaphore_wait(barrier, seqs - 1 + groups - 1)
        for j in range(inner):

            @pl.when(j != i)
            def _(j=j):
                if n == 0:
                    dec_copy(i, j).start()
                push_copy(n, i, j).start()

    gath[i] = push[:, pl.ds(pl.multiple_of(i * part, part), part), :]
    dgath[i] = dec[...]

    loads[3].wait()
    loads[4].wait()
    loads[5].wait()
    total = c[...]
    middle = total[tokens // 2 - 1 : tokens // 2]
    last = total[tokens - 1 : tokens]
    down = k[...].astype(F32) * jnp.exp(middle - total)
    kdn[...] = down.astype(BF16)
    scale[...] = jnp.exp(last - total)
    ktail[...] = down * jnp.exp(last - middle)

    def inside_block(h):
        at = cols[h]
        g_h = g[:, at]
        score = jnp.where(lower, product(g_h, v[:, at], 1, 1), 0.0).astype(BF16)
        total = c[:, at]
        middle = total[tokens // 2 - 1 : tokens // 2]
        from_start = product(twice(g_h, 1), both(s[h], 1), 1, 1) * jnp.exp(total)
        kdn_h = kdn[:, at]
        qup_h = qup[:, at]
        inside = product(score, kdn_h, 1, 0)
        back = product(score, qup_h, 0, 0)
        gq_out[:, at] = (jnp.exp(total - middle) * inside + from_start).astype(BF16)
        gk_part[:, at] = jnp.exp(middle - total) * back
        terms[:, at] = (
            qup_h.astype(F32) * inside - kdn_h.astype(F32) * back + q[:, at].astype(F32) * from_start
        )


    for h in range(half):
        inside_block(h)

    share = pl.ds(pl.multiple_of(i * part, part), part)

    def hop_copy(n):
        first, end = chunks[n]
        return pltpu.make_async_remote_copy(
            src_ref=leave.at[first:end],
            dst_ref=carry.at[first:end],
            send_sem=hop_s.at[n],
            recv_sem=hop_r.at[n],
            device_id=(p - inner, hd),
            device_id_type=MESH,
        )

    def end_copy(n, sender, to, where):
        first, end = chunks[n]
        return pltpu.make_async_remote_copy(
            src_ref=ends.at[to, first:end],
            dst_ref=incoming.at[first:end, where, :],
            send_sem=end_s.at[n, to],
            recv_sem=end_r.at[n, sender],
            device_id=(o * inner + to, hd),
            device_id_type=MESH,
        )

    def pass_on(n):
        for h in range(*chunks[n]):
            leave[h] = (
                alone[inner - 1, h] + decays[inner - 1, h, 0:1] * carry[h].astype(F32)
            ).astype(BF16)
        hop_copy(n).start()

    def hand_back(n):
        first, end = chunks[n]
        for h in range(first, end):
            from_later = carry[h].astype(F32)
            ends[inner - 1, h] = carry[h]
            for j in range(inner - 1):
                ends[j, h] = (alone[j, h] + decays[j, h, 0:1] * from_later).astype(BF16)
        for j in range(inner):

            @pl.when(j != i)
            def _(j=j):
                end_copy(n, i, j, share).start()

        incoming[first:end, share, :] = ends[i, first:end]

    @pl.when(o == outer - 1)
    def _():
        carry[...] = jnp.zeros_like(carry)

    for n, (first, end) in enumerate(chunks):
        for j in range(inner):

            @pl.when(j != i)
            def _(j=j):
                if n == 0:
                    dec_copy(j, j).wait_recv()
                push_copy(n, j, j).wait_recv()

        for h in range(first, end):
            state = gath[inner - 1, h].astype(F32)
            decay = dgath[inner - 1, h : h + 1]
            for j in range(inner - 2, -1, -1):
                alone[j, h] = state
                decays[j, h] = jnp.broadcast_to(decay, (8, LANES))
                step = dgath[j, h : h + 1]
                state = gath[j, h].astype(F32) + step * state
                decay = decay * step
            alone[inner - 1, h] = state
            decays[inner - 1, h] = jnp.broadcast_to(decay, (8, LANES))

        @pl.when(o == outer - 1)
        def _(n=n):
            if outer > 1:
                pass_on(n)
            hand_back(n)

    def values_part(h):
        at = cols[h]
        total = c[:, at]
        middle = total[tokens // 2 - 1 : tokens // 2]
        k_high, k_low = halves(k[:, at].astype(F32) * jnp.exp(middle - total))
        q_high, q_low = halves(q[:, at].astype(F32) * jnp.exp(total - middle))
        weight = product(
            jnp.concatenate([k_high, k_high], axis=1), jnp.concatenate([q_high, q_low], axis=1), 1, 1
        ) + product(k_low, q_high, 1, 1)
        weight = jnp.where(upper, weight, 0.0)
        gv_part[:, at] = product(both(weight, 1), twice(g[:, at], 0), 1, 0)

    loads[6].wait()

    @pl.when(p < seqs - 1)
    def _():
        before_copy().start()

    @pl.when(p == 0)
    def _():
        x[0:EDGE] = jnp.zeros((EDGE, columns), BF16)

    for h in range(half, heads):
        inside_block(h)
    for h in range(half):
        values_part(h)

    if outer > 1:

        @pl.when(o < outer - 1)
        def _():
            for n in range(len(chunks)):
                hop_copy(n).wait_recv()

                @pl.when(o > 0)
                def _(n=n):
                    pass_on(n)

                hand_back(n)

    for h in range(half, heads):
        values_part(h)
    for h in range(heads):
        turned[h] = s[h].T
        at = cols[h]
        tail_high, tail_low = halves(ktail[:, at])
        tails[h, :, 0:LANES] = tail_high
        tails[h, :, LANES:] = tail_low

    for n, (first, end) in enumerate(chunks):
        for j in range(inner):

            @pl.when(j != i)
            def _(j=j):
                end_copy(n, j, j, slice(j * part, (j + 1) * part)).wait_recv()

        for h in range(first, end):
            at = cols[h]
            gv[0:tokens, at] = (
                gv_part[:, at] + product(tails[h], twice(incoming[h], 1), 1, 1)
            ).astype(BF16)

    def edge_copy():
        return pltpu.make_async_remote_copy(
            src_ref=gv.at[0:EDGE],
            dst_ref=gv.at[tokens : tokens + EDGE],
            send_sem=edge_s,
            recv_sem=edge_r,
            device_id=(p - 1, hd),
            device_id_type=MESH,
        )

    @pl.when(p > 0)
    def _():
        edge_copy().start()
        before_copy().wait_recv()

    @pl.when(p == seqs - 1)
    def _():
        gv[tokens : tokens + EDGE] = jnp.zeros((EDGE, columns), BF16)

    rows = gv[0:tokens].astype(F32)
    x_f = x[...].astype(F32)
    for tap in range(taps):
        sums[tap : tap + 1] = jnp.sum(
            rows * x_f[EDGE - tap : EDGE - tap + tokens], axis=0, keepdims=True
        )

    def sum_copy(sender, to):
        return pltpu.make_async_remote_copy(
            src_ref=sums,
            dst_ref=all_sums.at[sender],
            send_sem=sum_s.at[to],
            recv_sem=sum_r.at[sender],
            device_id=(o * inner + to, hd),
            device_id_type=MESH,
        )

    def total_copy(sender, to):
        return pltpu.make_async_remote_copy(
            src_ref=group_sum,
            dst_ref=group_sums.at[sender],
            send_sem=total_s.at[to],
            recv_sem=total_r.at[sender],
            device_id=(to * inner + i, hd),
            device_id_type=MESH,
        )

    for j in range(inner):

        @pl.when(j != i)
        def _(j=j):
            sum_copy(i, j).start()

    all_sums[i] = sums[...]

    loads[7].wait()

    def convolve(first, end):
        rows = gv[first : end + EDGE].astype(F32)
        result = w[0:1] * rows[: end - first]
        for tap in range(1, taps):
            result = result + w[tap : tap + 1] * rows[tap : tap + end - first]
        gi[first:end] = result.astype(BF16)

    def row_copy(sender, to):
        return pltpu.make_async_remote_copy(
            src_ref=gi.at[to * own_rows : (to + 1) * own_rows],
            dst_ref=gi_out.at[:, pl.ds(pl.multiple_of(sender * columns, LANES), columns)],
            send_sem=row_s.at[to],
            recv_sem=row_r.at[sender],
            device_id=(p, to),
            device_id_type=MESH,
        )

    def keep_copy(to):
        return pltpu.make_async_copy(
            gi.at[to * own_rows : (to + 1) * own_rows], gi_out.at[:, mine], row_s.at[to]
        )

    def hand_out(to):
        @pl.when(to != hd)
        def _():
            row_copy(hd, to).start()

        @pl.when(to == hd)
        def _():
            keep_copy(to).start()

    for to in range(groups - 1):
        convolve(to * own_rows, (to + 1) * own_rows)
        hand_out(to)

    gg_part[...] = product(twice(upper_b, 1), both(terms[...], 0), 1, 0)

    def keys_and_gates(h):
        at = cols[h]
        later = product(v[:, at], incoming[h], 1, 0)
        gk_out[:, at] = (gk_part[:, at] + scale[:, at] * later).astype(BF16)
        own = jnp.sum(incoming[h].astype(F32) * turned[h], axis=0, keepdims=True)
        gg = (
            gg_part[:, at]
            + product(strict_b, (ktail[:, at] * later).astype(BF16), 1, 0)
            + own * dec[h : h + 1]
        )
        gg_out[:, at] = gg.astype(BF16)

    for h in range(half):
        keys_and_gates(h)

    @pl.when(p < seqs - 1)
    def _():
        edge_copy().wait_recv()

    convolve((groups - 1) * own_rows, tokens)
    hand_out(groups - 1)


    for j in range(inner):

        @pl.when(j != i)
        def _(j=j):
            sum_copy(j, j).wait_recv()

    added = all_sums[0]
    for j in range(1, inner):
        added = added + all_sums[j]
    group_sum[...] = added
    for n in range(outer):

        @pl.when(n != o)
        def _(n=n):
            total_copy(o, n).start()

    group_sums[o] = added
    for h in range(half, heads):
        keys_and_gates(h)
    for n in range(outer):

        @pl.when(n != o)
        def _(n=n):
            total_copy(n, n).wait_recv()

    added = group_sums[0]
    for n in range(1, outer):
        added = added + group_sums[n]
    gw_out[...] = added

    for sender in range(groups):

        @pl.when(sender != hd)
        def _(sender=sender):
            row_copy(sender, sender).wait_recv()

    for to in range(groups):

        @pl.when(to != hd)
        def _(to=to):
            row_copy(hd, to).wait_send()

        @pl.when(to == hd)
        def _(to=to):
            keep_copy(to).wait()

    for n in range(outer):

        @pl.when(n != o)
        def _(n=n):
            total_copy(o, n).wait_send()

    for j in range(inner):

        @pl.when(j != i)
        def _(j=j):
            dec_copy(i, j).wait_send()
            sum_copy(i, j).wait_send()
            for n in range(len(chunks)):
                push_copy(n, i, j).wait_send()
                end_copy(n, i, j, share).wait_send()

    if outer > 1:

        @pl.when(o > 0)
        def _():
            for n in range(len(chunks)):
                hop_copy(n).wait_send()

    @pl.when(p > 0)
    def _():
        edge_copy().wait_send()

    @pl.when(p < seqs - 1)
    def _():
        before_copy().wait_send()


def deliver(*refs):
    count = len(refs) // 2
    copies = [
        pltpu.make_async_copy(refs[n], refs[count + n], refs[-1].at[n]) for n in range(count)
    ]
    for copy in copies:
        copy.start()
    for copy in copies:
        copy.wait()


def solution(mesh):
    seqs, groups = mesh.shape["seq"], mesh.shape["head"]
    inner = 4 if seqs % 4 == 0 else 1

    def per_device(queries, key_rows, values, conv_input, log_gates, grad_output, saved_state, conv_kernel):
        tokens, columns = queries.shape
        heads = saved_state.shape[1]
        taps = conv_kernel.shape[0]
        part = LANES // inner
        flat = (tokens, columns)
        dma = pltpu.SemaphoreType.DMA
        vmem = pltpu.VMEM
        shapes = (
            jax.ShapeDtypeStruct(flat, BF16),
            jax.ShapeDtypeStruct(flat, BF16),
            jax.ShapeDtypeStruct(flat, BF16),
            jax.ShapeDtypeStruct((tokens // groups, columns * groups), BF16),
            jax.ShapeDtypeStruct((taps, columns), F32),
        )
        results = pl.pallas_call(
            functools.partial(body, seqs, groups, inner, heads, tokens, taps),
            out_shape=tuple(vmem(made.shape, made.dtype) for made in shapes),
            in_specs=[pl.BlockSpec(memory_space=pltpu.HBM)] * 8,
            out_specs=[pl.BlockSpec(memory_space=pltpu.VMEM)] * 5,
            scratch_shapes=[vmem(flat, BF16)] * 3
            + [vmem((tokens + EDGE, columns), BF16)]
            + [vmem(flat, BF16)] * 2
            + [
                vmem((heads, LANES, LANES), F32),
                vmem((taps, columns), F32),
                vmem((heads, LANES, LANES), F32),
                vmem((heads, tokens, 2 * LANES), BF16),
                vmem(flat, F32),
                vmem(flat, BF16),
                vmem(flat, BF16),
                vmem(flat, F32),
                vmem(flat, F32),
                vmem(flat, F32),
                vmem(flat, F32),
                vmem(flat, F32),
                vmem(flat, F32),
                vmem((heads, LANES, LANES), BF16),
                vmem((heads, LANES), F32),
                vmem((inner, heads, part, LANES), BF16),
                vmem((inner, heads, LANES), F32),
                vmem((inner, heads, part, LANES), F32),
                vmem((inner, heads, 8, LANES), F32),
                vmem((heads, part, LANES), BF16),
                vmem((heads, part, LANES), BF16),
                vmem((inner, heads, part, LANES), BF16),
                vmem((heads, LANES, LANES), BF16),
                vmem((tokens + EDGE, columns), BF16),
                vmem(flat, BF16),
                vmem((taps, columns), F32),
                vmem((inner, taps, columns), F32),
                vmem((taps, columns), F32),
                vmem((seqs // inner, taps, columns), F32),
                dma((8,)),
                dma((len(spans(heads)), inner)),
                dma((len(spans(heads)), inner)),
                dma((inner,)),
                dma((inner,)),
                dma((len(spans(heads)),)),
                dma((len(spans(heads)),)),
                dma((len(spans(heads)), inner)),
                dma((len(spans(heads)), inner)),
                dma,
                dma,
                dma,
                dma,
                dma((groups,)),
                dma((groups,)),
                dma((inner,)),
                dma((inner,)),
                dma((seqs // inner,)),
                dma((seqs // inner,)),
            ],
            compiler_params=pltpu.CompilerParams(
                collective_id=0, has_side_effects=True, vmem_limit_bytes=60 * 1024 * 1024
            ),
        )(queries, key_rows, values, conv_input, log_gates, grad_output, saved_state, conv_kernel)
        return pl.pallas_call(
            deliver,
            out_shape=shapes,
            in_specs=[pl.BlockSpec(memory_space=pltpu.VMEM)] * len(shapes),
            out_specs=[pl.BlockSpec(memory_space=pltpu.HBM)] * len(shapes),
            scratch_shapes=[dma((len(shapes),))],
            compiler_params=pltpu.CompilerParams(vmem_limit_bytes=2 * 1024 * 1024),
        )(*results)

    return jax.shard_map(
        per_device,
        mesh=mesh,
        in_specs=(
            P("seq", "head"),
            P("seq", "head"),
            P("seq", "head"),
            P("seq", "head"),
            P("seq", "head"),
            P("seq", "head"),
            P("seq", "head", None, None),
            P(),
        ),
        out_specs=(
            P("seq", "head"),
            P("seq", "head"),
            P("seq", "head"),
            P(("seq", "head"), None),
            P(None, "head"),
        ),
        check_vma=False,
    )
```

```python
import functools

import jax
import jax.numpy as jnp
from jax import lax
from jax.experimental import pallas as pl
from jax.experimental.pallas import tpu as pltpu
from jax.sharding import PartitionSpec as P

MESH = pl.DeviceIdType.MESH
F32 = jnp.float32
BF16 = jnp.bfloat16
LANES = 128
EDGE = 16


def product(a, b, dim_a, dim_b):
    return lax.dot_general(
        a, b, (((dim_a,), (dim_b,)), ((), ())), preferred_element_type=F32
    )


def halves(x):
    high = x.astype(BF16)
    return high, (x - high.astype(F32)).astype(BF16)


def both(x, axis):
    return jnp.concatenate(halves(x), axis=axis)


def twice(x, axis):
    return jnp.concatenate([x, x], axis=axis)


def spans(heads):
    count = 3 if heads % 3 == 0 else 1
    width = heads // count
    return [(n * width, (n + 1) * width) for n in range(count)]


def body(
    seqs, groups, inner, heads, tokens, taps,
    q_in, k_in, v_in, x_in, l_in, g_in, s_in, w_in,
    gq_out, gk_out, gg_out, gi_out, gw_out,
    q, k, v, x, l, g, s, w,
    turned, tails, c, qup, kdn, scale, ktail, terms, gk_part, gv_part, gg_part,
    push, dec, gath, dgath, alone, decays, carry, leave, ends, incoming,
    gv, gi, sums, all_sums, group_sum, group_sums,
    in_sem, push_s, push_r, dec_s, dec_r, hop_s, hop_r, end_s, end_r,
    before_s, before_r, edge_s, edge_r, row_s, row_r, sum_s, sum_r, total_s, total_r,
):
    p = lax.axis_index("seq")
    hd = lax.axis_index("head")
    o, i = p // inner, p % inner
    outer = seqs // inner
    part = LANES // inner
    columns = heads * LANES
    own_rows = tokens // groups
    half = heads // 2
    chunks = spans(heads)
    cols = [slice(h * LANES, (h + 1) * LANES) for h in range(heads)]

    mine = pl.ds(pl.multiple_of(hd * columns, LANES), columns)
    loads = [
        pltpu.make_async_copy(src, dst, in_sem.at[n])
        for n, (src, dst) in enumerate(
            [(l_in, l), (q_in, q), (g_in, g), (k_in, k), (v_in, v), (s_in.at[0], s), (x_in, x.at[EDGE:]), (w_in.at[:, mine], w)]
        )
    ]
    for load in loads:
        load.start()

    def greet(n, carried):
        pl.semaphore_signal(
            barrier, inc=1, device_id=(lax.rem(p + n, seqs), hd), device_id_type=MESH
        )
        return carried

    barrier = pltpu.get_barrier_semaphore()
    lax.fori_loop(1, seqs, greet, 0)
    for n in range(1, groups):
        pl.semaphore_signal(
            barrier, inc=1, device_id=(p, lax.rem(hd + n, groups)), device_id_type=MESH
        )

    row = lax.broadcasted_iota(jnp.int32, (tokens, tokens), 0)
    col = lax.broadcasted_iota(jnp.int32, (tokens, tokens), 1)
    lower = row >= col
    upper = col >= row
    lower_b = jnp.where(lower, 1.0, 0.0).astype(BF16)
    upper_b = jnp.where(upper, 1.0, 0.0).astype(BF16)
    strict_b = jnp.where(row > col, 1.0, 0.0).astype(BF16)

    loads[0].wait()
    total = product(lower_b, l[...], 1, 0)
    c[...] = total
    middle = total[tokens // 2 - 1 : tokens // 2]
    last = total[tokens - 1 : tokens]
    to_middle = jnp.exp(middle)
    grow = jnp.exp(total - middle)
    whole = jnp.exp(last)
    for h in range(heads):
        dec[h : h + 1] = whole[:, cols[h]]
    loads[1].wait()
    up = q[...].astype(F32) * grow
    qup[...] = up.astype(BF16)
    full = up * to_middle
    loads[2].wait()

    def push_copy(n, sender, to):
        first, end = chunks[n]
        return pltpu.make_async_remote_copy(
            src_ref=push.at[first:end, to * part : (to + 1) * part, :],
            dst_ref=gath.at[sender, first:end],
            send_sem=push_s.at[n, to],
            recv_sem=push_r.at[n, sender],
            device_id=(o * inner + to, hd),
            device_id_type=MESH,
        )

    def dec_copy(sender, to):
        return pltpu.make_async_remote_copy(
            src_ref=dec,
            dst_ref=dgath.at[sender],
            send_sem=dec_s.at[to],
            recv_sem=dec_r.at[sender],
            device_id=(o * inner + to, hd),
            device_id_type=MESH,
        )

    def before_copy():
        return pltpu.make_async_remote_copy(
            src_ref=x.at[tokens : tokens + EDGE],
            dst_ref=x.at[0:EDGE],
            send_sem=before_s,
            recv_sem=before_r,
            device_id=(p + 1, hd),
            device_id_type=MESH,
        )

    for n, (first, end) in enumerate(chunks):
        for h in range(first, end):
            push[h] = product(
                twice(g[:, cols[h]], 0), both(full[:, cols[h]], 0), 0, 0
            ).astype(BF16)
        if n == 0:
            pl.semaphore_wait(barrier, seqs - 1 + groups - 1)
        for j in range(inner):

            @pl.when(j != i)
            def _(j=j):
                if n == 0:
                    dec_copy(i, j).start()
                push_copy(n, i, j).start()

    gath[i] = push[:, pl.ds(pl.multiple_of(i * part, part), part), :]
    dgath[i] = dec[...]

    loads[3].wait()
    loads[4].wait()
    loads[5].wait()
    total = c[...]
    middle = total[tokens // 2 - 1 : tokens // 2]
    last = total[tokens - 1 : tokens]
    down = k[...].astype(F32) * jnp.exp(middle - total)
    kdn[...] = down.astype(BF16)
    scale[...] = jnp.exp(last - total)
    ktail[...] = down * jnp.exp(last - middle)

    def inside_block(h):
        at = cols[h]
        g_h = g[:, at]
        score = jnp.where(lower, product(g_h, v[:, at], 1, 1), 0.0).astype(BF16)
        total = c[:, at]
        middle = total[tokens // 2 - 1 : tokens // 2]
        from_start = product(twice(g_h, 1), both(s[h], 1), 1, 1) * jnp.exp(total)
        kdn_h = kdn[:, at]
        qup_h = qup[:, at]
        inside = product(score, kdn_h, 1, 0)
        back = product(score, qup_h, 0, 0)
        gq_out[:, at] = (jnp.exp(total - middle) * inside + from_start).astype(BF16)
        gk_part[:, at] = jnp.exp(middle - total) * back
        terms[:, at] = (
            qup_h.astype(F32) * inside - kdn_h.astype(F32) * back + q[:, at].astype(F32) * from_start
        )


    for h in range(half):
        inside_block(h)

    share = pl.ds(pl.multiple_of(i * part, part), part)

    def hop_copy(n):
        first, end = chunks[n]
        return pltpu.make_async_remote_copy(
            src_ref=leave.at[first:end],
            dst_ref=carry.at[first:end],
            send_sem=hop_s.at[n],
            recv_sem=hop_r.at[n],
            device_id=(p - inner, hd),
            device_id_type=MESH,
        )

    def end_copy(n, sender, to, where):
        first, end = chunks[n]
        return pltpu.make_async_remote_copy(
            src_ref=ends.at[to, first:end],
            dst_ref=incoming.at[first:end, where, :],
            send_sem=end_s.at[n, to],
            recv_sem=end_r.at[n, sender],
            device_id=(o * inner + to, hd),
            device_id_type=MESH,
        )

    def pass_on(n):
        for h in range(*chunks[n]):
            leave[h] = (
                alone[inner - 1, h] + decays[inner - 1, h, 0:1] * carry[h].astype(F32)
            ).astype(BF16)
        hop_copy(n).start()

    def hand_back(n):
        first, end = chunks[n]
        for h in range(first, end):
            from_later = carry[h].astype(F32)
            ends[inner - 1, h] = carry[h]
            for j in range(inner - 1):
                ends[j, h] = (alone[j, h] + decays[j, h, 0:1] * from_later).astype(BF16)
        for j in range(inner):

            @pl.when(j != i)
            def _(j=j):
                end_copy(n, i, j, share).start()

        incoming[first:end, share, :] = ends[i, first:end]

    @pl.when(o == outer - 1)
    def _():
        carry[...] = jnp.zeros_like(carry)

    for n, (first, end) in enumerate(chunks):
        for j in range(inner):

            @pl.when(j != i)
            def _(j=j):
                if n == 0:
                    dec_copy(j, j).wait_recv()
                push_copy(n, j, j).wait_recv()

        for h in range(first, end):
            state = gath[inner - 1, h].astype(F32)
            decay = dgath[inner - 1, h : h + 1]
            for j in range(inner - 2, -1, -1):
                alone[j, h] = state
                decays[j, h] = jnp.broadcast_to(decay, (8, LANES))
                step = dgath[j, h : h + 1]
                state = gath[j, h].astype(F32) + step * state
                decay = decay * step
            alone[inner - 1, h] = state
            decays[inner - 1, h] = jnp.broadcast_to(decay, (8, LANES))

        if outer > 1:

            @pl.when(o == outer - 1)
            def _(n=n):
                pass_on(n)

    def values_part(h):
        at = cols[h]
        total = c[:, at]
        middle = total[tokens // 2 - 1 : tokens // 2]
        k_high, k_low = halves(k[:, at].astype(F32) * jnp.exp(middle - total))
        q_high, q_low = halves(q[:, at].astype(F32) * jnp.exp(total - middle))
        weight = product(
            jnp.concatenate([k_high, k_high], axis=1), jnp.concatenate([q_high, q_low], axis=1), 1, 1
        ) + product(k_low, q_high, 1, 1)
        weight = jnp.where(upper, weight, 0.0)
        gv_part[:, at] = product(both(weight, 1), twice(g[:, at], 0), 1, 0)

    for h in range(half, heads):
        inside_block(h)

    @pl.when(o == outer - 1)
    def _():
        for n in range(len(chunks)):
            hand_back(n)

    for h in range(half):
        values_part(h)

    if outer > 1:

        @pl.when(o < outer - 1)
        def _():
            for n in range(len(chunks)):
                hop_copy(n).wait_recv()

                @pl.when(o > 0)
                def _(n=n):
                    pass_on(n)

                hand_back(n)

    loads[6].wait()

    @pl.when(p < seqs - 1)
    def _():
        before_copy().start()

    @pl.when(p == 0)
    def _():
        x[0:EDGE] = jnp.zeros((EDGE, columns), BF16)

    for h in range(half, heads):
        values_part(h)
    for h in range(heads):
        turned[h] = s[h].T
        at = cols[h]
        tail_high, tail_low = halves(ktail[:, at])
        tails[h, :, 0:LANES] = tail_high
        tails[h, :, LANES:] = tail_low

    for n, (first, end) in enumerate(chunks):
        for j in range(inner):

            @pl.when(j != i)
            def _(j=j):
                end_copy(n, j, j, slice(j * part, (j + 1) * part)).wait_recv()

        for h in range(first, end):
            at = cols[h]
            gv[0:tokens, at] = (
                gv_part[:, at] + product(tails[h], twice(incoming[h], 1), 1, 1)
            ).astype(BF16)

    def edge_copy():
        return pltpu.make_async_remote_copy(
            src_ref=gv.at[0:EDGE],
            dst_ref=gv.at[tokens : tokens + EDGE],
            send_sem=edge_s,
            recv_sem=edge_r,
            device_id=(p - 1, hd),
            device_id_type=MESH,
        )

    @pl.when(p > 0)
    def _():
        edge_copy().start()
        before_copy().wait_recv()

    @pl.when(p == seqs - 1)
    def _():
        gv[tokens : tokens + EDGE] = jnp.zeros((EDGE, columns), BF16)

    rows = gv[0:tokens].astype(F32)
    x_f = x[...].astype(F32)
    for tap in range(taps):
        sums[tap : tap + 1] = jnp.sum(
            rows * x_f[EDGE - tap : EDGE - tap + tokens], axis=0, keepdims=True
        )

    def sum_copy(sender, to):
        return pltpu.make_async_remote_copy(
            src_ref=sums,
            dst_ref=all_sums.at[sender],
            send_sem=sum_s.at[to],
            recv_sem=sum_r.at[sender],
            device_id=(o * inner + to, hd),
            device_id_type=MESH,
        )

    def total_copy(sender, to):
        return pltpu.make_async_remote_copy(
            src_ref=group_sum,
            dst_ref=group_sums.at[sender],
            send_sem=total_s.at[to],
            recv_sem=total_r.at[sender],
            device_id=(to * inner + i, hd),
            device_id_type=MESH,
        )

    for j in range(inner):

        @pl.when(j != i)
        def _(j=j):
            sum_copy(i, j).start()

    all_sums[i] = sums[...]

    loads[7].wait()

    def convolve(first, end):
        rows = gv[first : end + EDGE].astype(F32)
        result = w[0:1] * rows[: end - first]
        for tap in range(1, taps):
            result = result + w[tap : tap + 1] * rows[tap : tap + end - first]
        gi[first:end] = result.astype(BF16)

    def row_copy(sender, to):
        return pltpu.make_async_remote_copy(
            src_ref=gi.at[to * own_rows : (to + 1) * own_rows],
            dst_ref=gi_out.at[:, pl.ds(pl.multiple_of(sender * columns, LANES), columns)],
            send_sem=row_s.at[to],
            recv_sem=row_r.at[sender],
            device_id=(p, to),
            device_id_type=MESH,
        )

    def keep_copy(to):
        return pltpu.make_async_copy(
            gi.at[to * own_rows : (to + 1) * own_rows], gi_out.at[:, mine], row_s.at[to]
        )

    def hand_out(to):
        @pl.when(to != hd)
        def _():
            row_copy(hd, to).start()

        @pl.when(to == hd)
        def _():
            keep_copy(to).start()

    for to in range(groups - 1):
        convolve(to * own_rows, (to + 1) * own_rows)
        hand_out(to)

    gg_part[...] = product(twice(upper_b, 1), both(terms[...], 0), 1, 0)

    def keys_and_gates(h):
        at = cols[h]
        later = product(v[:, at], incoming[h], 1, 0)
        gk_out[:, at] = (gk_part[:, at] + scale[:, at] * later).astype(BF16)
        own = jnp.sum(incoming[h].astype(F32) * turned[h], axis=0, keepdims=True)
        gg = (
            gg_part[:, at]
            + product(strict_b, (ktail[:, at] * later).astype(BF16), 1, 0)
            + own * dec[h : h + 1]
        )
        gg_out[:, at] = gg.astype(BF16)

    for h in range(half):
        keys_and_gates(h)

    @pl.when(p < seqs - 1)
    def _():
        edge_copy().wait_recv()

    convolve((groups - 1) * own_rows, tokens)
    hand_out(groups - 1)


    for j in range(inner):

        @pl.when(j != i)
        def _(j=j):
            sum_copy(j, j).wait_recv()

    added = all_sums[0]
    for j in range(1, inner):
        added = added + all_sums[j]
    group_sum[...] = added
    for n in range(outer):

        @pl.when(n != o)
        def _(n=n):
            total_copy(o, n).start()

    group_sums[o] = added
    for h in range(half, heads):
        keys_and_gates(h)
    for n in range(outer):

        @pl.when(n != o)
        def _(n=n):
            total_copy(n, n).wait_recv()

    added = group_sums[0]
    for n in range(1, outer):
        added = added + group_sums[n]
    gw_out[...] = added

    for sender in range(groups):

        @pl.when(sender != hd)
        def _(sender=sender):
            row_copy(sender, sender).wait_recv()

    for to in range(groups):

        @pl.when(to != hd)
        def _(to=to):
            row_copy(hd, to).wait_send()

        @pl.when(to == hd)
        def _(to=to):
            keep_copy(to).wait()

    for n in range(outer):

        @pl.when(n != o)
        def _(n=n):
            total_copy(o, n).wait_send()

    for j in range(inner):

        @pl.when(j != i)
        def _(j=j):
            dec_copy(i, j).wait_send()
            sum_copy(i, j).wait_send()
            for n in range(len(chunks)):
                push_copy(n, i, j).wait_send()
                end_copy(n, i, j, share).wait_send()

    if outer > 1:

        @pl.when(o > 0)
        def _():
            for n in range(len(chunks)):
                hop_copy(n).wait_send()

    @pl.when(p > 0)
    def _():
        edge_copy().wait_send()

    @pl.when(p < seqs - 1)
    def _():
        before_copy().wait_send()


def deliver(*refs):
    count = len(refs) // 2
    copies = [
        pltpu.make_async_copy(refs[n], refs[count + n], refs[-1].at[n]) for n in range(count)
    ]
    for copy in copies:
        copy.start()
    for copy in copies:
        copy.wait()


def solution(mesh):
    seqs, groups = mesh.shape["seq"], mesh.shape["head"]
    inner = 4 if seqs % 4 == 0 else 1

    def per_device(queries, key_rows, values, conv_input, log_gates, grad_output, saved_state, conv_kernel):
        tokens, columns = queries.shape
        heads = saved_state.shape[1]
        taps = conv_kernel.shape[0]
        part = LANES // inner
        flat = (tokens, columns)
        dma = pltpu.SemaphoreType.DMA
        vmem = pltpu.VMEM
        shapes = (
            jax.ShapeDtypeStruct(flat, BF16),
            jax.ShapeDtypeStruct(flat, BF16),
            jax.ShapeDtypeStruct(flat, BF16),
            jax.ShapeDtypeStruct((tokens // groups, columns * groups), BF16),
            jax.ShapeDtypeStruct((taps, columns), F32),
        )
        results = pl.pallas_call(
            functools.partial(body, seqs, groups, inner, heads, tokens, taps),
            out_shape=tuple(vmem(made.shape, made.dtype) for made in shapes),
            in_specs=[pl.BlockSpec(memory_space=pltpu.HBM)] * 8,
            out_specs=[pl.BlockSpec(memory_space=pltpu.VMEM)] * 5,
            scratch_shapes=[vmem(flat, BF16)] * 3
            + [vmem((tokens + EDGE, columns), BF16)]
            + [vmem(flat, BF16)] * 2
            + [
                vmem((heads, LANES, LANES), F32),
                vmem((taps, columns), F32),
                vmem((heads, LANES, LANES), F32),
                vmem((heads, tokens, 2 * LANES), BF16),
                vmem(flat, F32),
                vmem(flat, BF16),
                vmem(flat, BF16),
                vmem(flat, F32),
                vmem(flat, F32),
                vmem(flat, F32),
                vmem(flat, F32),
                vmem(flat, F32),
                vmem(flat, F32),
                vmem((heads, LANES, LANES), BF16),
                vmem((heads, LANES), F32),
                vmem((inner, heads, part, LANES), BF16),
                vmem((inner, heads, LANES), F32),
                vmem((inner, heads, part, LANES), F32),
                vmem((inner, heads, 8, LANES), F32),
                vmem((heads, part, LANES), BF16),
                vmem((heads, part, LANES), BF16),
                vmem((inner, heads, part, LANES), BF16),
                vmem((heads, LANES, LANES), BF16),
                vmem((tokens + EDGE, columns), BF16),
                vmem(flat, BF16),
                vmem((taps, columns), F32),
                vmem((inner, taps, columns), F32),
                vmem((taps, columns), F32),
                vmem((seqs // inner, taps, columns), F32),
                dma((8,)),
                dma((len(spans(heads)), inner)),
                dma((len(spans(heads)), inner)),
                dma((inner,)),
                dma((inner,)),
                dma((len(spans(heads)),)),
                dma((len(spans(heads)),)),
                dma((len(spans(heads)), inner)),
                dma((len(spans(heads)), inner)),
                dma,
                dma,
                dma,
                dma,
                dma((groups,)),
                dma((groups,)),
                dma((inner,)),
                dma((inner,)),
                dma((seqs // inner,)),
                dma((seqs // inner,)),
            ],
            compiler_params=pltpu.CompilerParams(
                collective_id=0, has_side_effects=True, vmem_limit_bytes=60 * 1024 * 1024
            ),
        )(queries, key_rows, values, conv_input, log_gates, grad_output, saved_state, conv_kernel)
        return pl.pallas_call(
            deliver,
            out_shape=shapes,
            in_specs=[pl.BlockSpec(memory_space=pltpu.VMEM)] * len(shapes),
            out_specs=[pl.BlockSpec(memory_space=pltpu.HBM)] * len(shapes),
            scratch_shapes=[dma((len(shapes),))],
            compiler_params=pltpu.CompilerParams(vmem_limit_bytes=2 * 1024 * 1024),
        )(*results)

    return jax.shard_map(
        per_device,
        mesh=mesh,
        in_specs=(
            P("seq", "head"),
            P("seq", "head"),
            P("seq", "head"),
            P("seq", "head"),
            P("seq", "head"),
            P("seq", "head"),
            P("seq", "head", None, None),
            P(),
        ),
        out_specs=(
            P("seq", "head"),
            P("seq", "head"),
            P("seq", "head"),
            P(("seq", "head"), None),
            P(None, "head"),
        ),
        check_vma=False,
    )
```
